512 devices in a mesh: pipe: 32 (over y, z_lo, core), tp: 16 (over x, z_hi).
Axes of the slice: x: 4, y: 8, z: 8 (z_hi: 4, z_lo: 2; z = z_hi * 2 + z_lo), core: 2. Of those that a mesh axis runs over, the one named last changes fastest.
Arguments:
- act_in: bfloat16 [32, 256, 12288], P('pipe', None, 'tp'), may hold values from -8 to 8
- grad_in: bfloat16 [32, 256, 12288], P('pipe', None, 'tp'), may hold values from -6 to 6
- held: bfloat16 [32, 256, 12288], P('pipe', None, 'tp'), may hold values from -8 to 8
- park: int32 [32], replicated, may hold values from 0 to 1, as said below
- gain_q: float32 [32, 12288], P('pipe', 'tp'), may hold values from 0.5 to 1.5
- gain_k: float32 [32, 12288], P('pipe', 'tp'), may hold values from 0.5 to 1.5
- gain_v: float32 [32, 12288], P('pipe', 'tp'), may hold values from 0.5 to 1.5
Outputs:
- act_out: bfloat16 [32, 256, 12288], P('pipe', None, 'tp')
- grad_out: bfloat16 [32, 256, 12288], P('pipe', None, 'tp')
- held_out: bfloat16 [32, 256, 12288], P('pipe', None, 'tp')
The draws below stay inside these ranges and needn't reach their ends.
Inputs may be any that keep to these rules, and one draw needn't show every extreme that they name: park is 0 on sections 16 and higher; among the lower sections both values occur.
All inputs are finite; a program needn't handle non-finite values.
Results may differ from the reference program's by a relative error of at most 0.0042.
Values may be sent and summed in bfloat16 or wider, within the bound.
A program may use at most 64 MiB of HBM per device.

```python
import jax
import jax.numpy as jnp
from jax import lax

HD = 128
D = 12288
SEQ = 256
N_PIPE = 32


def draw_act_in(key, part):
    key = jax.random.fold_in(key, 11)
    base = jax.random.fold_in(key, 0)
    field = jax.random.normal(base, (N_PIPE, SEQ, D), jnp.float32)
    return jnp.clip(field, -8.0, 8.0).astype(jnp.bfloat16)


def draw_held(key, part):
    key = jax.random.fold_in(key, 23)
    base = jax.random.fold_in(key, 0)
    field = jax.random.normal(base, (N_PIPE, SEQ, D), jnp.float32)
    return jnp.clip(field, -8.0, 8.0).astype(jnp.bfloat16)


def draw_park(key, part):
    key = jax.random.fold_in(key, 37)
    coins = jax.random.randint(key, (N_PIPE,), 0, 2, dtype=jnp.int32)
    sections = jnp.arange(N_PIPE, dtype=jnp.int32)
    plan = jnp.where(sections < N_PIPE // 2, coins, 0)
    return plan.at[0].set(1).at[1].set(0)


def shard_levels(stream_key, dims, cuts, smallest, high):
    gain, own = 1.0, jax.random.fold_in(stream_key, 6)
    for dim, shards_of in cuts:
        draws = jnp.exp(jax.random.uniform(jax.random.fold_in(own, dim), (shards_of,), jnp.float32, smallest / len(cuts), high / len(cuts)))
        gain = gain * jnp.repeat(draws, dims[dim] // shards_of).reshape([-1 if axis == dim else 1 for axis in range(len(dims))])
    return gain


def normal_values(own_key, extent, width, reach, shards=(), kind=jnp.bfloat16):
    result = width * jax.random.normal(own_key, extent, jnp.float32)
    if shards:
        result = result * shard_levels(own_key, extent, shards, -0.22, 0.18)
    return jnp.clip(result, -reach, reach).astype(kind)


def setup_inputs(seed: int = 0) -> dict:
    key_of = jax.random.split(jax.random.key(seed), 8)
    act_in = draw_act_in(jax.random.fold_in(key_of[7], 71), 0)
    grad_in = normal_values(key_of[1], (N_PIPE, SEQ, D), 1.0, 6.0, ((0, 32), (2, 16)))
    held = draw_held(jax.random.fold_in(key_of[7], 71), 0)
    park = draw_park(jax.random.fold_in(key_of[7], 71), 0)
    gain_q = jnp.clip(1.0 + 0.1 * jax.random.normal(key_of[4], (N_PIPE, D), jnp.float32), 0.5, 1.5)
    gain_k = jnp.clip(1.0 + 0.1 * jax.random.normal(key_of[5], (N_PIPE, D), jnp.float32), 0.5, 1.5)
    gain_v = jnp.clip(1.0 + 0.1 * jax.random.normal(key_of[6], (N_PIPE, D), jnp.float32), 0.5, 1.5)
    return dict(act_in=act_in, grad_in=grad_in, held=held, park=park, gain_q=gain_q, gain_k=gain_k, gain_v=gain_v)


EPS = 1e-05

def normalize(x):
    xf = x.astype(jnp.float32)
    rate = lax.rsqrt(lax.optimization_barrier(jnp.mean(xf * xf, axis=-1, keepdims=True)) + EPS)
    return (xf, rate)

def heads_of(field):
    return field.reshape(field.shape[0], -1, HD)

def project(xf, rate, gain_q, gain_k, gain_v):
    normed = xf * rate
    query = (normed * gain_q).astype(jnp.bfloat16)
    keys = (normed * gain_k).astype(jnp.bfloat16)
    values = (normed * gain_v).astype(jnp.bfloat16)
    return (query, keys, values)

def softmax_of(query, keys):
    q_heads = heads_of(query).astype(jnp.float32)
    k_heads = heads_of(keys).astype(jnp.float32)
    raw = jnp.einsum('shd,thd->hst', q_heads, k_heads, precision=lax.Precision.HIGHEST) * HD ** (-0.5)
    positions = jnp.arange(raw.shape[1], dtype=jnp.int32)
    causal = positions[:, None] >= positions[None, :]
    raw = jnp.where(causal[None], raw, -jnp.inf)
    top = lax.optimization_barrier(jnp.max(raw, axis=-1, keepdims=True))
    powers = jnp.exp(raw - top)
    return powers / lax.optimization_barrier(jnp.sum(powers, axis=-1, keepdims=True))

def forward(x, gain_q, gain_k, gain_v):
    xf, rate = normalize(x)
    query, keys, values = project(xf, rate, gain_q, gain_k, gain_v)
    probs = softmax_of(query, keys)
    probs_b = lax.optimization_barrier(probs.astype(jnp.bfloat16)).astype(jnp.float32)
    mixed = jnp.einsum('hst,thd->shd', probs_b, heads_of(values).astype(jnp.float32), precision=lax.Precision.HIGHEST)
    return (xf + mixed.reshape(xf.shape)).astype(jnp.bfloat16)

def backward(x, grad, gain_q, gain_k, gain_v):
    xf, rate = normalize(x)
    query, keys, values = project(xf, rate, gain_q, gain_k, gain_v)
    probs = softmax_of(query, keys)
    probs_b = lax.optimization_barrier(probs.astype(jnp.bfloat16)).astype(jnp.float32)
    g_heads = heads_of(grad).astype(jnp.float32)
    q_heads = heads_of(query).astype(jnp.float32)
    k_heads = heads_of(keys).astype(jnp.float32)
    v_heads = heads_of(values).astype(jnp.float32)
    dval = jnp.einsum('hst,shd->thd', probs_b, g_heads, precision=lax.Precision.HIGHEST)
    dprob = jnp.einsum('shd,thd->hst', g_heads, v_heads, precision=lax.Precision.HIGHEST)
    delta = lax.optimization_barrier(jnp.sum(probs * dprob, axis=-1, keepdims=True))
    dscore = (probs * (dprob - delta) * HD ** (-0.5)).astype(jnp.bfloat16)
    dscore = lax.optimization_barrier(dscore).astype(jnp.float32)
    dquery = jnp.einsum('hst,thd->shd', dscore, k_heads, precision=lax.Precision.HIGHEST)
    dkeys = jnp.einsum('hst,shd->thd', dscore, q_heads, precision=lax.Precision.HIGHEST)
    dnorm = dquery.reshape(xf.shape) * gain_q + dkeys.reshape(xf.shape) * gain_k + dval.reshape(xf.shape) * gain_v
    total = lax.optimization_barrier(jnp.sum(dnorm * xf, axis=-1, keepdims=True)) / D
    dinput = rate * dnorm - xf * rate * rate * rate * total
    return (grad.astype(jnp.float32) + dinput).astype(jnp.bfloat16)

def reference(act_in, grad_in, held, park, gain_q, gain_k, gain_v):
    sections = jnp.arange(N_PIPE, dtype=jnp.int32)

    def run_forward(index):
        return forward(act_in[index], gain_q[index], gain_k[index], gain_v[index])
    mirrored = held[::-1]

    def run_backward(index):
        return backward(mirrored[index], grad_in[index], gain_q[index], gain_k[index], gain_v[index])
    outputs = lax.map(run_forward, sections)
    grads = lax.map(run_backward, sections)
    zeros = jnp.zeros_like(act_in[:1])
    act_out = jnp.concatenate([zeros, outputs[:-1]], axis=0)
    grad_out = jnp.concatenate([grads[1:], zeros], axis=0)
    held_out = jnp.where((park[::-1] == 1)[:, None, None], act_in[::-1], held)
    return (act_out, grad_out, held_out)
```

```python
import jax
import jax.numpy as jnp
from jax import lax
from jax.experimental import pallas as pl
from jax.experimental.pallas import tpu as pltpu
from jax.sharding import PartitionSpec as P

HD = 128
SEQ = 256
EPS = 1e-05
MESH = pl.DeviceIdType.MESH
F32 = jnp.float32
BF16 = jnp.bfloat16
SCALE = HD ** (-0.5)


def nt(a, b):
    return lax.dot_general(a, b, (((1,), (1,)), ((), ())), preferred_element_type=F32)


def tn(a, b):
    return lax.dot_general(a, b, (((0,), (0,)), ((), ())), preferred_element_type=F32)


def nn(a, b):
    return lax.dot_general(a, b, (((1,), (0,)), ((), ())), preferred_element_type=F32)


def row_sums(field):
    ones = jnp.ones((8, HD), F32)
    sums = lax.dot_general(
        ones, field, (((1,), (1,)), ((), ())),
        precision=lax.Precision.HIGHEST, preferred_element_type=F32,
    )
    return sums[0:1, 0:128], sums[0:1, 128:256]


def as_column(row):
    return jnp.transpose(jnp.broadcast_to(row, (128, 128)))


def softmax_rows(raw, first_row):
    rows = lax.broadcasted_iota(jnp.int32, raw.shape, 0) + first_row
    columns = lax.broadcasted_iota(jnp.int32, raw.shape, 1)
    raw = jnp.where(rows >= columns, raw * SCALE, -jnp.inf)
    top = jnp.max(raw, axis=-1, keepdims=True)
    powers = jnp.exp(raw - top)
    return powers * (1.0 / jnp.sum(powers, axis=-1, keepdims=True))


def kernel(
    heads, sections, width,
    act, grad, held, gq, gk, gv,
    act_out, grad_out, far,
    xs, gs, hs, ss, ys, dns, rate_f, rate_s, total_b, tacc,
    msg1, gat1, msg2, gat2, rmsg, rget,
    load_x, load_g, load_h, held_send, held_recv, y_send, y_recv, b_send, b_recv,
    far_send, far_recv, s1, r1, s2, r2, rs, rr, zsem,
):
    section = lax.axis_index("pipe")
    me = lax.axis_index("tp")
    mirror = sections - 1 - section
    nxt = section + 1
    prv = section - 1
    half = sections // 2
    features = width * heads * HD
    low = section < half
    first = section == 0
    last = section == sections - 1

    def cols(h):
        return pl.ds(pl.multiple_of(h * HD, HD), HD)

    def load(h, src, dst, sem):
        return pltpu.make_async_copy(src.at[0, :, cols(h)], dst.at[h], sem.at[h])

    def start_loads(h, c):
        load(h, act, xs, load_x).start()
        load(h, grad, gs, load_g).start()
        return c

    hload = pltpu.make_async_copy(held.at[0], hs, load_h)
    lax.fori_loop(0, heads, start_loads, 0)
    hload.start()

    barrier = pltpu.get_barrier_semaphore()

    def greet(p, c):
        pl.semaphore_signal(
            barrier, inc=1, device_id=(section, lax.rem(me + p, width)), device_id_type=MESH
        )
        return c

    pl.semaphore_signal(barrier, inc=1, device_id=(mirror, me), device_id_type=MESH)

    @pl.when(jnp.logical_not(last))
    def _():
        pl.semaphore_signal(barrier, inc=1, device_id=(nxt, me), device_id_type=MESH)

    @pl.when(jnp.logical_not(first))
    def _():
        pl.semaphore_signal(barrier, inc=1, device_id=(prv, me), device_id_type=MESH)

    lax.fori_loop(1, width, greet, 0)
    edge = jnp.where(jnp.logical_or(first, last), 1, 0)
    pl.semaphore_wait(barrier, width + 2 - edge)

    def held_copy(h):
        return pltpu.make_async_remote_copy(
            src_ref=held.at[0, :, cols(h)], dst_ref=ss.at[h],
            send_sem=held_send.at[h], recv_sem=held_recv.at[h],
            device_id=(mirror, me), device_id_type=MESH,
        )

    def start_held(h, c):
        held_copy(h).start()
        return c

    lax.fori_loop(0, heads, start_held, 0)

    def wait_loads(h, c):
        load(h, act, xs, load_x).wait()
        return c

    lax.fori_loop(0, heads, wait_loads, 0)

    def x_squares(h, acc):
        v = xs[h].astype(F32)
        return acc + v * v

    sq_x = lax.fori_loop(0, heads, x_squares, jnp.zeros((SEQ, HD), F32))
    hload.wait()

    def h_squares(h, acc):
        v = hs[:, cols(h)].astype(F32)
        return acc + v * v

    sq_h = lax.fori_loop(0, heads, h_squares, jnp.zeros((SEQ, HD), F32))
    a0, a1 = row_sums(sq_x)
    b0, b1 = row_sums(sq_h)
    parts = jnp.concatenate([a0, a1, b0, b1, jnp.zeros((4, 128), F32)], axis=0)
    msg1[...] = parts
    gat1[pl.ds(me, 1)] = parts[None]

    def exchange(msg, gat, ssem, rsem):
        def copy(p):
            return pltpu.make_async_remote_copy(
                src_ref=msg, dst_ref=gat.at[me],
                send_sem=ssem.at[p], recv_sem=rsem.at[p],
                device_id=(section, lax.rem(me + p, width)), device_id_type=MESH,
            )

        def start(p, c):
            copy(p).start()
            return c

        def wait(p, c):
            copy(p).wait()
            return c

        lax.fori_loop(1, width, start, 0)
        lax.fori_loop(1, width, wait, 0)
        return jnp.sum(gat[...], axis=0)

    sums = exchange(msg1, gat1, s1, r1)
    rates = lax.rsqrt(sums / features + EPS)
    rmsg[...] = rates
    rate_copy = pltpu.make_async_remote_copy(
        src_ref=rmsg, dst_ref=rget, send_sem=rs, recv_sem=rr,
        device_id=(mirror, me), device_id_type=MESH,
    )
    rate_copy.start()
    rate_f[pl.ds(0, 128)] = as_column(rates[0:1])
    rate_f[pl.ds(128, 128)] = as_column(rates[1:2])

    def project(xf, rate, h):
        normed = xf * rate
        return (
            (normed * gq[:, cols(h)]).astype(BF16),
            (normed * gk[:, cols(h)]).astype(BF16),
            (normed * gv[:, cols(h)]).astype(BF16),
        )

    def y_copy(h):
        return pltpu.make_async_remote_copy(
            src_ref=ys.at[h], dst_ref=act_out.at[0, :, cols(h)],
            send_sem=y_send.at[h], recv_sem=y_recv.at[h],
            device_id=(jnp.minimum(nxt, sections - 1), me), device_id_type=MESH,
        )

    def forward(h, c):
        xf = xs[h].astype(F32)
        q, k, v = project(xf, rate_f[...], h)
        p0 = softmax_rows(nt(q[0:128], k[0:128]), 0).astype(BF16)
        p1 = softmax_rows(nt(q[128:256], k), 128).astype(BF16)
        ys[h, pl.ds(0, 128)] = (xf[0:128] + nn(p0, v[0:128])).astype(BF16)
        ys[h, pl.ds(128, 128)] = (xf[128:256] + nn(p1, v)).astype(BF16)

        @pl.when(jnp.logical_not(last))
        def _():
            y_copy(h).start()

        return c

    lax.fori_loop(0, heads, forward, 0)

    rate_copy.wait()
    got = rget[...]
    rate_s[pl.ds(0, 128)] = as_column(got[2:3])
    rate_s[pl.ds(128, 128)] = as_column(got[3:4])
    tacc[...] = jnp.zeros((SEQ, HD), F32)

    def act_copy(h):
        return pltpu.make_async_remote_copy(
            src_ref=act.at[0, :, cols(h)], dst_ref=far.at[0, :, cols(h)],
            send_sem=far_send.at[h], recv_sem=far_recv.at[h],
            device_id=(mirror, me), device_id_type=MESH,
        )

    def backward(h, c):
        load(h, grad, gs, load_g).wait()
        held_copy(h).wait()

        @pl.when(low)
        def _():
            act_copy(h).start()

        xf = ss[h].astype(F32)
        q, k, v = project(xf, rate_s[...], h)
        g = gs[h]
        p0 = softmax_rows(nt(q[0:128], k[0:128]), 0)
        p1 = softmax_rows(nt(q[128:256], k), 128)
        d0 = nt(g[0:128], v[0:128])
        d1 = nt(g[128:256], v)

        def dscore(probs, dprob):
            delta = jnp.sum(probs * dprob, axis=-1, keepdims=True)
            return (probs * (dprob - delta) * SCALE).astype(BF16)

        e0 = dscore(p0, d0)
        e1 = dscore(p1, d1)
        dval = tn(p1.astype(BF16), g[128:256])
        dkey = tn(e1, q[128:256])
        dval0 = dval[0:128] + tn(p0.astype(BF16), g[0:128])
        dkey0 = dkey[0:128] + tn(e0, q[0:128])
        g_q, g_k, g_v = gq[:, cols(h)], gk[:, cols(h)], gv[:, cols(h)]
        dn0 = nn(e0, k[0:128]) * g_q + dkey0 * g_k + dval0 * g_v
        dn1 = nn(e1, k) * g_q + dkey[128:256] * g_k + dval[128:256] * g_v
        dns[h, pl.ds(0, 128)] = dn0
        dns[h, pl.ds(128, 128)] = dn1
        tacc[pl.ds(0, 128)] += dn0 * xf[0:128]
        tacc[pl.ds(128, 128)] += dn1 * xf[128:256]
        return c

    lax.fori_loop(0, heads, backward, 0)

    t0, t1 = row_sums(tacc[...])
    parts2 = jnp.concatenate([t0, t1, jnp.zeros((6, 128), F32)], axis=0)
    msg2[...] = parts2
    gat2[pl.ds(me, 1)] = parts2[None]
    totals = exchange(msg2, gat2, s2, r2) / features
    total_b[pl.ds(0, 128)] = as_column(totals[0:1])
    total_b[pl.ds(128, 128)] = as_column(totals[1:2])
    rate = rate_s[...]
    total_b[...] = total_b[...] * (rate * rate * rate)

    def b_copy(h):
        return pltpu.make_async_remote_copy(
            src_ref=gs.at[h], dst_ref=grad_out.at[0, :, cols(h)],
            send_sem=b_send.at[h], recv_sem=b_recv.at[h],
            device_id=(jnp.maximum(prv, 0), me), device_id_type=MESH,
        )

    def finish(h, c):
        dx = rate_s[...] * dns[h] - ss[h].astype(F32) * total_b[...]
        gs[h] = (gs[h].astype(F32) + dx).astype(BF16)

        @pl.when(jnp.logical_not(first))
        def _():
            b_copy(h).start()

        return c

    lax.fori_loop(0, heads, finish, 0)

    @pl.when(jnp.logical_or(first, last))
    def _():
        hs[...] = jnp.zeros(hs.shape, BF16)

    @pl.when(first)
    def _():
        copy = pltpu.make_async_copy(hs, act_out.at[0], zsem)
        copy.start()
        copy.wait()

    @pl.when(last)
    def _():
        copy = pltpu.make_async_copy(hs, grad_out.at[0], zsem)
        copy.start()
        copy.wait()

    def drain(h, c):
        @pl.when(jnp.logical_not(last))
        def _():
            y_copy(h).wait_send()
            b_copy(h).wait_recv()

        @pl.when(jnp.logical_not(first))
        def _():
            y_copy(h).wait_recv()
            b_copy(h).wait_send()

        @pl.when(low)
        def _():
            act_copy(h).wait_send()

        @pl.when(jnp.logical_not(low))
        def _():
            act_copy(h).wait_recv()

        return c

    lax.fori_loop(0, heads, drain, 0)


def solution(mesh):
    sections, width = mesh.shape["pipe"], mesh.shape["tp"]

    def shards(act_in, grad_in, held, park, gain_q, gain_k, gain_v):
        heads = act_in.shape[2] // HD
        block = jax.ShapeDtypeStruct(act_in.shape, BF16)
        hbm = pl.BlockSpec(memory_space=pl.ANY)
        vmem = pl.BlockSpec(memory_space=pltpu.VMEM)
        dma = pltpu.SemaphoreType.DMA

        def body(*refs):
            kernel(heads, sections, width, *refs)

        act_out, grad_out, far = pl.pallas_call(
            body,
            out_shape=(block, block, block),
            in_specs=[hbm, hbm, hbm, vmem, vmem, vmem],
            out_specs=(hbm, hbm, hbm),
            scratch_shapes=[
                pltpu.VMEM((heads, SEQ, HD), BF16),
                pltpu.VMEM((heads, SEQ, HD), BF16),
                pltpu.VMEM((SEQ, heads * HD), BF16),
                pltpu.VMEM((heads, SEQ, HD), BF16),
                pltpu.VMEM((heads, SEQ, HD), BF16),
                pltpu.VMEM((heads, SEQ, HD), F32),
                pltpu.VMEM((SEQ, HD), F32),
                pltpu.VMEM((SEQ, HD), F32),
                pltpu.VMEM((SEQ, HD), F32),
                pltpu.VMEM((SEQ, HD), F32),
                pltpu.VMEM((8, 128), F32),
                pltpu.VMEM((width, 8, 128), F32),
                pltpu.VMEM((8, 128), F32),
                pltpu.VMEM((width, 8, 128), F32),
                pltpu.VMEM((8, 128), F32),
                pltpu.VMEM((8, 128), F32),
                dma((heads,)), dma((heads,)), dma,
                dma((heads,)), dma((heads,)), dma((heads,)), dma((heads,)),
                dma((heads,)), dma((heads,)), dma((heads,)), dma((heads,)),
                dma((width,)), dma((width,)), dma((width,)), dma((width,)),
                dma, dma, dma,
            ],
            compiler_params=pltpu.CompilerParams(
                collective_id=0, has_side_effects=True, vmem_limit_bytes=24 * 1024 * 1024
            ),
            name="relay_tick",
        )(act_in, grad_in, held, gain_q, gain_k, gain_v)
        section = lax.axis_index("pipe")
        flag = jnp.take(park, sections - 1 - section)
        held_out = jnp.where(flag == 1, far, held)
        return act_out, grad_out, held_out

    wide = P("pipe", None, "tp")
    gain = P("pipe", "tp")
    return jax.shard_map(
        shards,
        mesh=mesh,
        in_specs=(wide, wide, wide, P(), gain, gain, gain),
        out_specs=(wide, wide, wide),
        check_vma=False,
    )
```

```python
import jax
import jax.numpy as jnp
from jax import lax
from jax.experimental import pallas as pl
from jax.experimental.pallas import tpu as pltpu
from jax.sharding import PartitionSpec as P

HD = 128
SEQ = 256
EPS = 1e-05
MESH = pl.DeviceIdType.MESH
F32 = jnp.float32
BF16 = jnp.bfloat16
SCALE = HD ** (-0.5)
FIRST = 2


def nt(a, b):
    return lax.dot_general(a, b, (((1,), (1,)), ((), ())), preferred_element_type=F32)


def tn(a, b):
    return lax.dot_general(a, b, (((0,), (0,)), ((), ())), preferred_element_type=F32)


def nn(a, b):
    return lax.dot_general(a, b, (((1,), (0,)), ((), ())), preferred_element_type=F32)


def row_sums(field):
    ones = jnp.ones((8, HD), F32)
    sums = lax.dot_general(
        ones, field, (((1,), (1,)), ((), ())),
        precision=lax.Precision.HIGHEST, preferred_element_type=F32,
    )
    return sums[0:1, 0:128], sums[0:1, 128:256]


def as_column(row):
    return jnp.transpose(jnp.broadcast_to(row, (128, 128)))


def softmax_rows(raw, first_row):
    rows = lax.broadcasted_iota(jnp.int32, raw.shape, 0) + first_row
    columns = lax.broadcasted_iota(jnp.int32, raw.shape, 1)
    raw = jnp.where(rows >= columns, raw * SCALE, -jnp.inf)
    top = jnp.max(raw, axis=-1, keepdims=True)
    powers = jnp.exp(raw - top)
    return powers * (1.0 / jnp.sum(powers, axis=-1, keepdims=True))


def kernel(
    heads, sections, width,
    act, grad, held, park, gq_in, gk_in, gv_in,
    act_out, grad_out, held_out,
    xs, gs, hs, ss, ys, xn, zs, far, gq, gk, gv, flags,
    rate_f, rate_s, tacc,
    msg1, gat1, msg3, gat3, hsum, hsum_got, esum, esum_got, rate_e, rate_e_got, bo, ho,
    load_x, load_g, load_h, load_p, load_w,
    held_send, held_recv, y_send, y_recv, b_send, b_recv, far_send, far_recv,
    s1, r1, s3, r3, hs_send, hs_recv, es, er, rs, rr, ho_sem, zero_sem,
    hello, near,
):
    section = lax.axis_index("pipe")
    me = lax.axis_index("tp")
    mirror = sections - 1 - section
    nxt = jnp.minimum(section + 1, sections - 1)
    prv = jnp.maximum(section - 1, 0)
    features = width * heads * HD
    odd = lax.rem(section, 2) == 1
    even = lax.rem(section, 2) == 0
    first = section == 0
    last = section == sections - 1
    half = sections // 2
    low = section < half
    inner = jnp.logical_and(section >= half // 4, section < half - half // 4)
    depth = lax.rem(me, 4)
    act_first = jnp.logical_and(low, jnp.logical_not(inner))
    act_mid = jnp.logical_and(inner, depth < 1)
    act_aft = jnp.logical_and(inner, jnp.logical_and(depth >= 1, depth < 1))
    act_later = jnp.logical_and(inner, jnp.logical_and(depth >= 1, depth >= 1))

    def cols(h):
        return pl.ds(pl.multiple_of(h * HD, HD), HD)

    def each_head(f):
        def step(h, c):
            f(h)
            return c

        lax.fori_loop(0, heads, step, 0)

    def each_peer(start, f):
        def step(p, c):
            f(p)
            return c

        lax.fori_loop(start, width, step, 0)

    def remote(src, dst, send, recv, device):
        return pltpu.make_async_remote_copy(
            src_ref=src, dst_ref=dst, send_sem=send, recv_sem=recv,
            device_id=device, device_id_type=MESH,
        )

    def signal(sem, device):
        pl.semaphore_signal(sem, inc=1, device_id=device, device_id_type=MESH)

    def held_copy(h):
        return remote(held.at[0, :, cols(h)], ss.at[h], held_send.at[h], held_recv.at[h], (mirror, me))

    def act_copy(h):
        return remote(act.at[0, :, cols(h)], far.at[h], far_send.at[h], far_recv.at[h], (mirror, me))

    def y_copy(h):
        return remote(ys.at[h], act_out.at[0, :, cols(h)], y_send.at[h], y_recv.at[h], (nxt, me))

    def b_copy(h):
        return remote(bo.at[h], grad_out.at[0, :, cols(h)], b_send.at[h], b_recv.at[h], (prv, me))

    def sum_copy(msg, gat, send, recv, p):
        return remote(msg, gat.at[me], send.at[p], recv.at[p], (section, lax.rem(me + p, width)))

    def total_copy(p):
        return remote(msg3, gat3.at[me], s3.at[p], r3.at[p], (section, lax.rem(me + p, width)))

    hsum_copy = remote(hsum, hsum_got, hs_send, hs_recv, (mirror, me))
    esum_copy = remote(esum, esum_got, es, er, (nxt, me))
    rate_copy = remote(rate_e, rate_e_got, rs, rr, (prv, me))

    barrier = pltpu.get_barrier_semaphore()

    @pl.when(odd)
    def _():
        signal(barrier, (mirror, me))
        signal(barrier, (prv, me))

        @pl.when(jnp.logical_not(last))
        def _():
            signal(barrier, (nxt, me))

        each_peer(1, lambda p: signal(barrier, (section, lax.rem(me + p, width))))

    load_held = pltpu.make_async_copy(held.at[0], hs, load_h)
    load_act = pltpu.make_async_copy(act.at[0], xs, load_x)
    load_grad = pltpu.make_async_copy(grad.at[0], gs, load_g)
    load_park = pltpu.make_async_copy(park, flags, load_p)
    load_gains = [
        pltpu.make_async_copy(src, dst, load_w.at[i])
        for i, (src, dst) in enumerate(((gq_in, gq), (gk_in, gk), (gv_in, gv)))
    ]
    load_held.start()
    load_act.start()
    load_grad.start()
    for copy in load_gains:
        copy.start()
    load_park.start()

    def squares(ref):
        def step(h, acc):
            v = ref[:, cols(h)].astype(F32)
            return acc + v * v

        return row_sums(lax.fori_loop(0, heads, step, jnp.zeros((SEQ, HD), F32)))

    load_held.wait()
    b0, b1 = squares(hs)
    hsum[0:1] = b0
    hsum[1:2] = b1

    def start_acts():
        @pl.when(act_first)
        def _():
            each_head(lambda h: act_copy(h).start())

    def start_some(h, c):
        held_copy(h).start()
        return c

    @pl.when(even)
    def _():
        pl.semaphore_wait(barrier, jnp.where(first, 2, 3))
        signal(hello, (mirror, me))
        signal(hello, (nxt, me))

        @pl.when(jnp.logical_not(first))
        def _():
            signal(hello, (prv, me))

        hsum_copy.start()
        lax.fori_loop(0, min(FIRST, heads), start_some, 0)
        pl.semaphore_wait(near, 1)
        lax.fori_loop(min(FIRST, heads), heads, start_some, 0)
        start_acts()

    @pl.when(odd)
    def _():
        pl.semaphore_wait(hello, jnp.where(last, 2, 3))
        hsum_copy.start()
        signal(near, (prv, me))
        lax.fori_loop(0, heads, start_some, 0)
        start_acts()

    load_act.wait()
    a0, a1 = squares(xs)
    for copy in load_gains:
        copy.wait()
    load_park.wait()
    flag = flags[mirror]

    @pl.when(even)
    def _():
        esum[0:1] = a0
        esum[1:2] = a1
        hsum_copy.wait_recv()
        esum[2:4] = hsum_got[...]
        esum_copy.start()
        rate_copy.wait_recv()

    @pl.when(odd)
    def _():
        pl.semaphore_wait(barrier, width - 1)
        msg1[0:1] = a0
        msg1[1:2] = a1
        hsum_copy.wait_recv()
        msg1[2:4] = hsum_got[...]
        esum_copy.wait_recv()
        msg1[4:8] = esum_got[...]
        each_peer(1, lambda p: sum_copy(msg1, gat1, s1, r1, p).start())
        gat1[pl.ds(me, 1)] = msg1[...][None]
        each_peer(1, lambda p: sum_copy(msg1, gat1, s1, r1, p).wait_recv())
        rates = lax.rsqrt(jnp.sum(gat1[...], axis=0) / features + EPS)
        rate_e[...] = rates[4:8]
        rate_copy.start()
        rate_e_got[...] = rates[0:4]

    rates = rate_e_got[...]
    rate_f[pl.ds(0, 128)] = as_column(rates[0:1])
    rate_f[pl.ds(128, 128)] = as_column(rates[1:2])
    rate_s[pl.ds(0, 128)] = as_column(rates[2:3])
    rate_s[pl.ds(128, 128)] = as_column(rates[3:4])

    def project(xf, rate, h):
        normed = xf * rate
        return (
            (normed * gq[:, cols(h)]).astype(BF16),
            (normed * gk[:, cols(h)]).astype(BF16),
            (normed * gv[:, cols(h)]).astype(BF16),
        )

    tacc[...] = jnp.zeros((SEQ, HD), F32)

    def backward(h):
        held_copy(h).wait_recv()

        xf = ss[h].astype(F32)
        rate = rate_s[...]
        q, k, v = project(xf, rate, h)
        g = gs[:, cols(h)]
        p0 = softmax_rows(nt(q[0:128], k[0:128]), 0)
        p1 = softmax_rows(nt(q[128:256], k), 128)
        d0 = nt(g[0:128], v[0:128])
        d1 = nt(g[128:256], v)

        def dscore(probs, dprob):
            delta = jnp.sum(probs * dprob, axis=-1, keepdims=True)
            return (probs * (dprob - delta) * SCALE).astype(BF16)

        e0 = dscore(p0, d0)
        e1 = dscore(p1, d1)
        dval = tn(p1.astype(BF16), g[128:256])
        dkey = tn(e1, q[128:256])
        dval0 = dval[0:128] + tn(p0.astype(BF16), g[0:128])
        dkey0 = dkey[0:128] + tn(e0, q[0:128])
        g_q, g_k, g_v = gq[:, cols(h)], gk[:, cols(h)], gv[:, cols(h)]
        dn0 = nn(e0, k[0:128]) * g_q + dkey0 * g_k + dval0 * g_v
        dn1 = nn(e1, k) * g_q + dkey[128:256] * g_k + dval[128:256] * g_v
        zs[h, pl.ds(0, 128)] = g[0:128].astype(F32) + rate[0:128] * dn0
        zs[h, pl.ds(128, 128)] = g[128:256].astype(F32) + rate[128:256] * dn1
        tacc[pl.ds(0, 128)] += dn0 * xf[0:128]
        tacc[pl.ds(128, 128)] += dn1 * xf[128:256]

    @pl.when(act_mid)
    def _():
        each_head(lambda h: act_copy(h).start())

    load_grad.wait()
    each_head(backward)

    t0, t1 = row_sums(tacc[...])
    msg3[0:1] = t0
    msg3[1:2] = t1
    each_peer(1, lambda p: total_copy(p).start())
    gat3[pl.ds(me, 1)] = msg3[...][None]

    @pl.when(act_aft)
    def _():
        each_head(lambda h: act_copy(h).start())

    def forward(h):
        xf = xs[:, cols(h)].astype(F32)
        q, k, v = project(xf, rate_f[...], h)
        p0 = softmax_rows(nt(q[0:128], k[0:128]), 0).astype(BF16)
        p1 = softmax_rows(nt(q[128:256], k), 128).astype(BF16)
        ys[h, pl.ds(0, 128)] = (xf[0:128] + nn(p0, v[0:128])).astype(BF16)
        ys[h, pl.ds(128, 128)] = (xf[128:256] + nn(p1, v)).astype(BF16)

        @pl.when(jnp.logical_not(last))
        def _():
            y_copy(h).start()

    each_head(forward)

    @pl.when(act_later)
    def _():
        each_head(lambda h: act_copy(h).start())

    def zero_grad(h):
        return pltpu.make_async_copy(xn.at[h], grad_out.at[0, :, cols(h)], zero_sem.at[h])

    def held_place(h):
        return pltpu.make_async_copy(ho.at[h], held_out.at[0, :, cols(h)], ho_sem.at[h])

    each_peer(1, lambda p: total_copy(p).wait_recv())
    totals = jnp.sum(gat3[...], axis=0) / features
    rate_f[pl.ds(0, 128)] = as_column(totals[0:1])
    rate_f[pl.ds(128, 128)] = as_column(totals[1:2])
    rate = rate_s[...]
    rate_f[...] = rate_f[...] * (rate * rate * rate)

    def finish(h):
        bo[h] = (zs[h] - ss[h].astype(F32) * rate_f[...]).astype(BF16)

        @pl.when(jnp.logical_not(first))
        def _():
            b_copy(h).start()

    each_head(finish)

    @pl.when(last)
    def _():
        def zero(h):
            xn[h] = jnp.zeros((SEQ, HD), BF16)
            zero_grad(h).start()

        each_head(zero)

    def zero_place(h):
        return pltpu.make_async_copy(xn.at[h], act_out.at[0, :, cols(h)], zero_sem.at[h])

    @pl.when(first)
    def _():
        def zero(h):
            xn[h] = jnp.zeros((SEQ, HD), BF16)
            zero_place(h).start()

        each_head(zero)

    def place(h):
        @pl.when(jnp.logical_not(low))
        def _():
            act_copy(h).wait_recv()

        mine = hs[:, cols(h)]

        @pl.when(low)
        def _():
            ho[h] = mine

        @pl.when(jnp.logical_not(low))
        def _():
            ho[h] = jnp.where(flag == 1, far[h], mine)

        held_place(h).start()

    each_head(place)

    def drain(h):
        held_place(h).wait()
        held_copy(h).wait_send()

        @pl.when(first)
        def _():
            zero_place(h).wait()

        @pl.when(last)
        def _():
            zero_grad(h).wait()

        @pl.when(low)
        def _():
            act_copy(h).wait_send()

        @pl.when(jnp.logical_not(last))
        def _():
            y_copy(h).wait_send()
            b_copy(h).wait_recv()

        @pl.when(jnp.logical_not(first))
        def _():
            y_copy(h).wait_recv()
            b_copy(h).wait_send()

    each_head(drain)

    each_peer(1, lambda p: total_copy(p).wait_send())

    hsum_copy.wait_send()

    @pl.when(even)
    def _():
        esum_copy.wait_send()

    @pl.when(odd)
    def _():
        each_peer(1, lambda p: sum_copy(msg1, gat1, s1, r1, p).wait_send())
        rate_copy.wait_send()


def place_kernel(a, b, c, a_out, b_out, c_out, a_mid, b_mid, c_mid, sems):
    stages = ((a, a_mid, a_out), (b, b_mid, b_out), (c, c_mid, c_out))
    into = [pltpu.make_async_copy(src, mid, sems.at[0, i]) for i, (src, mid, _) in enumerate(stages)]
    outof = [pltpu.make_async_copy(mid, dst, sems.at[1, i]) for i, (_, mid, dst) in enumerate(stages)]
    for copy in into:
        copy.start()
    for first, second in zip(into, outof):
        first.wait()
        second.start()
    for copy in outof:
        copy.wait()


def solution(mesh):
    sections, width = mesh.shape["pipe"], mesh.shape["tp"]

    def shards(act_in, grad_in, held, park, gain_q, gain_k, gain_v):
        heads = act_in.shape[2] // HD
        block = jax.ShapeDtypeStruct(act_in.shape, BF16)
        hbm = pl.BlockSpec(memory_space=pltpu.HBM)
        dma = pltpu.SemaphoreType.DMA

        def body(*refs):
            kernel(heads, sections, width, *refs)

        per_head = [dma((heads,)), dma((heads,))]
        per_peer = [dma((width,)), dma((width,))]
        field = pltpu.VMEM((SEQ, HD), F32)
        rows = pltpu.VMEM((4, 128), F32)
        pair = pltpu.VMEM((2, 128), F32)
        gathered = pltpu.VMEM((width, 4, 128), F32)
        flat = pltpu.VMEM((SEQ, heads * HD), BF16)
        stack = pltpu.VMEM((heads, SEQ, HD), BF16)
        wide_stack = pltpu.VMEM((heads, SEQ, HD), F32)
        gain_row = pltpu.VMEM((1, heads * HD), F32)
        outs = pl.pallas_call(
            body,
            out_shape=(block, block, block),
            in_specs=[hbm] * 7,
            out_specs=(hbm, hbm, hbm),
            scratch_shapes=[
                flat, flat, flat, stack, stack, stack,
                wide_stack, stack,
                gain_row, gain_row, gain_row, pltpu.SMEM((sections,), jnp.int32),
                field, field, field,
                pltpu.VMEM((8, 128), F32), pltpu.VMEM((width, 8, 128), F32), rows, gathered,
                pair, pair, rows, rows, rows, rows,
                stack, stack,
                dma, dma, dma, dma, dma((3,)),
                *per_head, *per_head, *per_head, *per_head,
                *per_peer, *per_peer,
                dma, dma, dma, dma, dma, dma,
                dma((heads,)), dma((heads,)),
                pltpu.SemaphoreType.REGULAR, pltpu.SemaphoreType.REGULAR,
            ],
            compiler_params=pltpu.CompilerParams(
                collective_id=0, has_side_effects=True, vmem_limit_bytes=56 * 1024 * 1024
            ),
            name="relay_tick",
        )(act_in, grad_in, held, park, gain_q, gain_k, gain_v)
        return pl.pallas_call(
            place_kernel,
            out_shape=(block, block, block),
            in_specs=[hbm] * 3,
            out_specs=(hbm, hbm, hbm),
            scratch_shapes=[pltpu.VMEM(block.shape, BF16)] * 3 + [dma((2, 3))],
            compiler_params=pltpu.CompilerParams(vmem_limit_bytes=56 * 1024 * 1024),
            name="place",
        )(*outs)

    wide = P("pipe", None, "tp")
    gain = P("pipe", "tp")
    return jax.shard_map(
        shards,
        mesh=mesh,
        in_specs=(wide, wide, wide, P(), gain, gain, gain),
        out_specs=(wide, wide, wide),
        check_vma=False,
    )
```

```python
import jax
import jax.numpy as jnp
from jax import lax
from jax.experimental import pallas as pl
from jax.experimental.pallas import tpu as pltpu
from jax.sharding import PartitionSpec as P

HD = 128
SEQ = 256
EPS = 1e-05
MESH = pl.DeviceIdType.MESH
F32 = jnp.float32
BF16 = jnp.bfloat16
SCALE = HD ** (-0.5)
FIRST = 2


def nt(a, b):
    return lax.dot_general(a, b, (((1,), (1,)), ((), ())), preferred_element_type=F32)


def tn(a, b):
    return lax.dot_general(a, b, (((0,), (0,)), ((), ())), preferred_element_type=F32)


def nn(a, b):
    return lax.dot_general(a, b, (((1,), (0,)), ((), ())), preferred_element_type=F32)


def row_sums(field):
    ones = jnp.ones((8, HD), F32)
    sums = lax.dot_general(
        ones, field, (((1,), (1,)), ((), ())),
        precision=lax.Precision.HIGHEST, preferred_element_type=F32,
    )
    return sums[0:1, 0:128], sums[0:1, 128:256]


def as_column(row):
    return jnp.transpose(jnp.broadcast_to(row, (128, 128)))


def softmax_rows(raw, first_row):
    rows = lax.broadcasted_iota(jnp.int32, raw.shape, 0) + first_row
    columns = lax.broadcasted_iota(jnp.int32, raw.shape, 1)
    raw = jnp.where(rows >= columns, raw * SCALE, -jnp.inf)
    top = jnp.max(raw, axis=-1, keepdims=True)
    powers = jnp.exp(raw - top)
    return powers * (1.0 / jnp.sum(powers, axis=-1, keepdims=True))


def kernel(
    heads, sections, width,
    act, grad, held, park, gq_in, gk_in, gv_in,
    act_out, grad_out, held_out,
    xs, gs, hs, ss, ys, xn, zs, far, gq, gk, gv, flags,
    rate_f, rate_s, tacc,
    msg1, gat1, msg3, gat3, msg4, gat4, hsum, hsum_got, esum, esum_got, rate_e, rate_e_got, bo, ho,
    load_x, load_g, load_h, load_p, load_w,
    held_send, held_recv, y_send, y_recv, b_send, b_recv, far_send, far_recv,
    s1, r1, s3, r3, hs_send, hs_recv, es, er, rs, rr, ho_sem, zero_sem,
    hello, near,
):
    section = lax.axis_index("pipe")
    me = lax.axis_index("tp")
    mirror = sections - 1 - section
    nxt = jnp.minimum(section + 1, sections - 1)
    prv = jnp.maximum(section - 1, 0)
    features = width * heads * HD
    odd = lax.rem(section, 2) == 1
    even = lax.rem(section, 2) == 0
    first = section == 0
    last = section == sections - 1
    half = sections // 2
    low = section < half
    inner = jnp.logical_and(section >= half // 4, section < half - half // 4)
    depth = lax.rem(me, 4)
    act_first = jnp.logical_and(low, jnp.logical_not(inner))
    act_mid = jnp.logical_and(inner, depth < 2)
    act_aft = jnp.logical_and(inner, jnp.logical_and(depth >= 2, depth < 2))
    act_later = jnp.logical_and(inner, jnp.logical_and(depth >= 2, depth >= 2))

    def cols(h):
        return pl.ds(pl.multiple_of(h * HD, HD), HD)

    def each_head(f):
        def step(h, c):
            f(h)
            return c

        lax.fori_loop(0, heads, step, 0)

    def each_peer(start, f):
        def step(p, c):
            f(p)
            return c

        lax.fori_loop(start, width, step, 0)

    def remote(src, dst, send, recv, device):
        return pltpu.make_async_remote_copy(
            src_ref=src, dst_ref=dst, send_sem=send, recv_sem=recv,
            device_id=device, device_id_type=MESH,
        )

    def signal(sem, device):
        pl.semaphore_signal(sem, inc=1, device_id=device, device_id_type=MESH)

    def held_copy(h):
        return remote(held.at[0, :, cols(h)], ss.at[h], held_send.at[h], held_recv.at[h], (mirror, me))

    def act_copy(h):
        return remote(act.at[0, :, cols(h)], far.at[h], far_send.at[h], far_recv.at[h], (mirror, me))

    def y_copy(h):
        return remote(ys.at[h], act_out.at[0, :, cols(h)], y_send.at[h], y_recv.at[h], (nxt, me))

    def b_copy(h):
        return remote(bo.at[h], grad_out.at[0, :, cols(h)], b_send.at[h], b_recv.at[h], (prv, me))

    def sum_copy(msg, gat, send, recv, p):
        return remote(msg, gat.at[me], send.at[p], recv.at[p], (section, lax.rem(me + p, width)))

    row, spot = me // 4, lax.rem(me, 4)

    def along_x(p):
        return remote(msg3, gat3.at[row], s3.at[p], r3.at[p], (section, lax.rem(row + p, 4) * 4 + spot))

    def along_z(p):
        return remote(msg4, gat4.at[spot], s3.at[p + 4], r3.at[p + 4], (section, row * 4 + lax.rem(spot + p, 4)))

    hsum_copy = remote(hsum, hsum_got, hs_send, hs_recv, (mirror, me))
    esum_copy = remote(esum, esum_got, es, er, (nxt, me))
    rate_copy = remote(rate_e, rate_e_got, rs, rr, (prv, me))

    barrier = pltpu.get_barrier_semaphore()

    @pl.when(odd)
    def _():
        signal(barrier, (mirror, me))
        signal(barrier, (prv, me))

        @pl.when(jnp.logical_not(last))
        def _():
            signal(barrier, (nxt, me))

        each_peer(1, lambda p: signal(barrier, (section, lax.rem(me + p, width))))

    load_held = pltpu.make_async_copy(held.at[0], hs, load_h)
    load_act = pltpu.make_async_copy(act.at[0], xs, load_x)
    load_grad = pltpu.make_async_copy(grad.at[0], gs, load_g)
    load_park = pltpu.make_async_copy(park, flags, load_p)
    load_gains = [
        pltpu.make_async_copy(src, dst, load_w.at[i])
        for i, (src, dst) in enumerate(((gq_in, gq), (gk_in, gk), (gv_in, gv)))
    ]
    load_held.start()
    load_act.start()
    load_grad.start()
    for copy in load_gains:
        copy.start()
    load_park.start()

    def squares(ref):
        def step(h, acc):
            v = ref[:, cols(h)].astype(F32)
            return acc + v * v

        return row_sums(lax.fori_loop(0, heads, step, jnp.zeros((SEQ, HD), F32)))

    load_held.wait()
    b0, b1 = squares(hs)
    hsum[0:1] = b0
    hsum[1:2] = b1

    def start_acts():
        @pl.when(act_first)
        def _():
            each_head(lambda h: act_copy(h).start())

    def start_some(h, c):
        held_copy(h).start()
        return c

    @pl.when(even)
    def _():
        pl.semaphore_wait(barrier, jnp.where(first, 2, 3))
        signal(hello, (mirror, me))
        signal(hello, (nxt, me))

        @pl.when(jnp.logical_not(first))
        def _():
            signal(hello, (prv, me))

        hsum_copy.start()
        lax.fori_loop(0, min(FIRST, heads), start_some, 0)
        pl.semaphore_wait(near, 1)
        lax.fori_loop(min(FIRST, heads), heads, start_some, 0)
        start_acts()

    @pl.when(odd)
    def _():
        pl.semaphore_wait(hello, jnp.where(last, 2, 3))
        hsum_copy.start()
        signal(near, (prv, me))
        lax.fori_loop(0, heads, start_some, 0)
        start_acts()

    load_act.wait()
    a0, a1 = squares(xs)
    for copy in load_gains:
        copy.wait()
    load_park.wait()
    flag = flags[mirror]

    @pl.when(even)
    def _():
        esum[0:1] = a0
        esum[1:2] = a1
        hsum_copy.wait_recv()
        esum[2:4] = hsum_got[...]
        esum_copy.start()
        rate_copy.wait_recv()

    @pl.when(odd)
    def _():
        pl.semaphore_wait(barrier, width - 1)
        msg1[0:1] = a0
        msg1[1:2] = a1
        hsum_copy.wait_recv()
        msg1[2:4] = hsum_got[...]
        esum_copy.wait_recv()
        msg1[4:8] = esum_got[...]
        each_peer(1, lambda p: sum_copy(msg1, gat1, s1, r1, p).start())
        gat1[pl.ds(me, 1)] = msg1[...][None]
        each_peer(1, lambda p: sum_copy(msg1, gat1, s1, r1, p).wait_recv())
        rates = lax.rsqrt(jnp.sum(gat1[...], axis=0) / features + EPS)
        rate_e[...] = rates[4:8]
        rate_copy.start()
        rate_e_got[...] = rates[0:4]

    rates = rate_e_got[...]
    rate_f[pl.ds(0, 128)] = as_column(rates[0:1])
    rate_f[pl.ds(128, 128)] = as_column(rates[1:2])
    rate_s[pl.ds(0, 128)] = as_column(rates[2:3])
    rate_s[pl.ds(128, 128)] = as_column(rates[3:4])

    def project(xf, rate, h):
        normed = xf * rate
        return (
            (normed * gq[:, cols(h)]).astype(BF16),
            (normed * gk[:, cols(h)]).astype(BF16),
            (normed * gv[:, cols(h)]).astype(BF16),
        )

    tacc[...] = jnp.zeros((SEQ, HD), F32)

    def backward(h):
        held_copy(h).wait_recv()

        xf = ss[h].astype(F32)
        rate = rate_s[...]
        q, k, v = project(xf, rate, h)
        g = gs[:, cols(h)]
        p0 = softmax_rows(nt(q[0:128], k[0:128]), 0)
        p1 = softmax_rows(nt(q[128:256], k), 128)
        d0 = nt(g[0:128], v[0:128])
        d1 = nt(g[128:256], v)

        def dscore(probs, dprob):
            delta = jnp.sum(probs * dprob, axis=-1, keepdims=True)
            return (probs * (dprob - delta) * SCALE).astype(BF16)

        e0 = dscore(p0, d0)
        e1 = dscore(p1, d1)
        dval = tn(p1.astype(BF16), g[128:256])
        dkey = tn(e1, q[128:256])
        dval0 = dval[0:128] + tn(p0.astype(BF16), g[0:128])
        dkey0 = dkey[0:128] + tn(e0, q[0:128])
        g_q, g_k, g_v = gq[:, cols(h)], gk[:, cols(h)], gv[:, cols(h)]
        dn0 = nn(e0, k[0:128]) * g_q + dkey0 * g_k + dval0 * g_v
        dn1 = nn(e1, k) * g_q + dkey[128:256] * g_k + dval[128:256] * g_v
        zs[h, pl.ds(0, 128)] = g[0:128].astype(F32) + rate[0:128] * dn0
        zs[h, pl.ds(128, 128)] = g[128:256].astype(F32) + rate[128:256] * dn1
        tacc[pl.ds(0, 128)] += dn0 * xf[0:128]
        tacc[pl.ds(128, 128)] += dn1 * xf[128:256]

    @pl.when(act_mid)
    def _():
        each_head(lambda h: act_copy(h).start())

    load_grad.wait()
    each_head(backward)

    t0, t1 = row_sums(tacc[...])
    msg3[0:1] = t0
    msg3[1:2] = t1
    for p in range(1, 4):
        along_x(p).start()
    gat3[pl.ds(row, 1)] = msg3[...][None]
    @pl.when(act_aft)
    def _():
        each_head(lambda h: act_copy(h).start())

    def forward(h):
        xf = xs[:, cols(h)].astype(F32)
        q, k, v = project(xf, rate_f[...], h)
        p0 = softmax_rows(nt(q[0:128], k[0:128]), 0).astype(BF16)
        p1 = softmax_rows(nt(q[128:256], k), 128).astype(BF16)
        ys[h, pl.ds(0, 128)] = (xf[0:128] + nn(p0, v[0:128])).astype(BF16)
        ys[h, pl.ds(128, 128)] = (xf[128:256] + nn(p1, v)).astype(BF16)

        @pl.when(jnp.logical_not(last))
        def _():
            y_copy(h).start()

    lax.fori_loop(0, 3, lambda h, c: (forward(h), c)[1], 0)

    for p in range(1, 4):
        along_x(p).wait_recv()
    mid = jnp.sum(gat3[...], axis=0)
    msg4[...] = mid
    for p in range(1, 4):
        along_z(p).start()
    gat4[pl.ds(spot, 1)] = mid[None]

    lax.fori_loop(3, heads, lambda h, c: (forward(h), c)[1], 0)

    @pl.when(act_later)
    def _():
        each_head(lambda h: act_copy(h).start())

    def zero_grad(h):
        return pltpu.make_async_copy(xn.at[h], grad_out.at[0, :, cols(h)], zero_sem.at[h])

    def held_place(h):
        return pltpu.make_async_copy(ho.at[h], held_out.at[0, :, cols(h)], ho_sem.at[h])

    for p in range(1, 4):
        along_z(p).wait_recv()
    totals = jnp.sum(gat4[...], axis=0) / features
    rate_f[pl.ds(0, 128)] = as_column(totals[0:1])
    rate_f[pl.ds(128, 128)] = as_column(totals[1:2])
    rate = rate_s[...]
    rate_f[...] = rate_f[...] * (rate * rate * rate)

    def finish(h):
        bo[h] = (zs[h] - ss[h].astype(F32) * rate_f[...]).astype(BF16)

        @pl.when(jnp.logical_not(first))
        def _():
            b_copy(h).start()

    each_head(finish)

    @pl.when(last)
    def _():
        def zero(h):
            xn[h] = jnp.zeros((SEQ, HD), BF16)
            zero_grad(h).start()

        each_head(zero)

    def zero_place(h):
        return pltpu.make_async_copy(xn.at[h], act_out.at[0, :, cols(h)], zero_sem.at[h])

    @pl.when(first)
    def _():
        def zero(h):
            xn[h] = jnp.zeros((SEQ, HD), BF16)
            zero_place(h).start()

        each_head(zero)

    def place(h):
        @pl.when(jnp.logical_not(low))
        def _():
            act_copy(h).wait_recv()

        mine = hs[:, cols(h)]

        @pl.when(low)
        def _():
            ho[h] = mine

        @pl.when(jnp.logical_not(low))
        def _():
            ho[h] = jnp.where(flag == 1, far[h], mine)

        held_place(h).start()

    each_head(place)

    def drain(h):
        held_place(h).wait()
        held_copy(h).wait_send()

        @pl.when(first)
        def _():
            zero_place(h).wait()

        @pl.when(last)
        def _():
            zero_grad(h).wait()

        @pl.when(low)
        def _():
            act_copy(h).wait_send()

        @pl.when(jnp.logical_not(last))
        def _():
            y_copy(h).wait_send()
            b_copy(h).wait_recv()

        @pl.when(jnp.logical_not(first))
        def _():
            y_copy(h).wait_recv()
            b_copy(h).wait_send()

    each_head(drain)

    for p in range(1, 4):
        along_x(p).wait_send()
        along_z(p).wait_send()

    hsum_copy.wait_send()

    @pl.when(even)
    def _():
        esum_copy.wait_send()

    @pl.when(odd)
    def _():
        each_peer(1, lambda p: sum_copy(msg1, gat1, s1, r1, p).wait_send())
        rate_copy.wait_send()


def place_kernel(a, b, c, a_out, b_out, c_out, a_mid, b_mid, c_mid, sems):
    stages = ((a, a_mid, a_out), (b, b_mid, b_out), (c, c_mid, c_out))
    into = [pltpu.make_async_copy(src, mid, sems.at[0, i]) for i, (src, mid, _) in enumerate(stages)]
    outof = [pltpu.make_async_copy(mid, dst, sems.at[1, i]) for i, (_, mid, dst) in enumerate(stages)]
    for copy in into:
        copy.start()
    for first, second in zip(into, outof):
        first.wait()
        second.start()
    for copy in outof:
        copy.wait()


def solution(mesh):
    sections, width = mesh.shape["pipe"], mesh.shape["tp"]

    def shards(act_in, grad_in, held, park, gain_q, gain_k, gain_v):
        heads = act_in.shape[2] // HD
        block = jax.ShapeDtypeStruct(act_in.shape, BF16)
        hbm = pl.BlockSpec(memory_space=pltpu.HBM)
        dma = pltpu.SemaphoreType.DMA

        def body(*refs):
            kernel(heads, sections, width, *refs)

        per_head = [dma((heads,)), dma((heads,))]
        per_peer = [dma((width,)), dma((width,))]
        field = pltpu.VMEM((SEQ, HD), F32)
        rows = pltpu.VMEM((4, 128), F32)
        pair = pltpu.VMEM((2, 128), F32)
        four = pltpu.VMEM((4, 2, 128), F32)
        flat = pltpu.VMEM((SEQ, heads * HD), BF16)
        stack = pltpu.VMEM((heads, SEQ, HD), BF16)
        wide_stack = pltpu.VMEM((heads, SEQ, HD), F32)
        gain_row = pltpu.VMEM((1, heads * HD), F32)
        outs = pl.pallas_call(
            body,
            out_shape=(block, block, block),
            in_specs=[hbm] * 7,
            out_specs=(hbm, hbm, hbm),
            scratch_shapes=[
                flat, flat, flat, stack, stack, stack,
                wide_stack, stack,
                gain_row, gain_row, gain_row, pltpu.SMEM((sections,), jnp.int32),
                field, field, field,
                pltpu.VMEM((8, 128), F32), pltpu.VMEM((width, 8, 128), F32), pair, four, pair, four,
                pair, pair, rows, rows, rows, rows,
                stack, stack,
                dma, dma, dma, dma, dma((3,)),
                *per_head, *per_head, *per_head, *per_head,
                *per_peer, *per_peer,
                dma, dma, dma, dma, dma, dma,
                dma((heads,)), dma((heads,)),
                pltpu.SemaphoreType.REGULAR, pltpu.SemaphoreType.REGULAR,
            ],
            compiler_params=pltpu.CompilerParams(
                collective_id=0, has_side_effects=True, vmem_limit_bytes=56 * 1024 * 1024
            ),
            name="relay_tick",
        )(act_in, grad_in, held, park, gain_q, gain_k, gain_v)
        return pl.pallas_call(
            place_kernel,
            out_shape=(block, block, block),
            in_specs=[hbm] * 3,
            out_specs=(hbm, hbm, hbm),
            scratch_shapes=[pltpu.VMEM(block.shape, BF16)] * 3 + [dma((2, 3))],
            compiler_params=pltpu.CompilerParams(vmem_limit_bytes=56 * 1024 * 1024),
            name="place",
        )(*outs)

    wide = P("pipe", None, "tp")
    gain = P("pipe", "tp")
    return jax.shard_map(
        shards,
        mesh=mesh,
        in_specs=(wide, wide, wide, P(), gain, gain, gain),
        out_specs=(wide, wide, wide),
        check_vma=False,
    )
```

```python
import jax
import jax.numpy as jnp
from jax import lax
from jax.experimental import pallas as pl
from jax.experimental.pallas import tpu as pltpu
from jax.sharding import PartitionSpec as P

HD = 128
SEQ = 256
EPS = 1e-05
MESH = pl.DeviceIdType.MESH
F32 = jnp.float32
BF16 = jnp.bfloat16
SCALE = HD ** (-0.5)
FIRST_MIDDLE = 1
FIRST_BEHIND = 4


def nt(a, b):
    return lax.dot_general(a, b, (((1,), (1,)), ((), ())), preferred_element_type=F32)


def tn(a, b):
    return lax.dot_general(a, b, (((0,), (0,)), ((), ())), preferred_element_type=F32)


def nn(a, b):
    return lax.dot_general(a, b, (((1,), (0,)), ((), ())), preferred_element_type=F32)


def row_sums(field):
    ones = jnp.ones((8, HD), F32)
    sums = lax.dot_general(
        ones, field, (((1,), (1,)), ((), ())),
        precision=lax.Precision.HIGHEST, preferred_element_type=F32,
    )
    return sums[0:1, 0:128], sums[0:1, 128:256]


def as_column(row):
    return jnp.transpose(jnp.broadcast_to(row, (128, 128)))


def softmax_rows(raw, first_row):
    rows = lax.broadcasted_iota(jnp.int32, raw.shape, 0) + first_row
    columns = lax.broadcasted_iota(jnp.int32, raw.shape, 1)
    raw = jnp.where(rows >= columns, raw * SCALE, -jnp.inf)
    top = jnp.max(raw, axis=-1, keepdims=True)
    powers = jnp.exp(raw - top)
    return powers * (1.0 / jnp.sum(powers, axis=-1, keepdims=True))


def kernel(
    heads, sections, width,
    act, grad, held, park, gq_in, gk_in, gv_in,
    act_out, grad_out, held_out,
    xs, gs, hs, ss, ys, xn, zs, far, gq, gk, gv, flags,
    rate_f, rate_s, tacc,
    msg1, gat1, msg3, gat3, msg4, gat4, hsum, hsum_got, esum, esum_got, rate_e, rate_e_got, bo, ho,
    load_x, load_g, load_h, load_p, load_w,
    held_send, held_recv, y_send, y_recv, b_send, b_recv, far_send, far_recv,
    s1, r1, s3, r3, hs_send, hs_recv, es, er, rs, rr, ho_sem, zero_sem,
    hello, near,
):
    section = lax.axis_index("pipe")
    me = lax.axis_index("tp")
    mirror = sections - 1 - section
    nxt = jnp.minimum(section + 1, sections - 1)
    prv = jnp.maximum(section - 1, 0)
    features = width * heads * HD
    odd = lax.rem(section, 2) == 1
    even = lax.rem(section, 2) == 0
    first = section == 0
    last = section == sections - 1
    half = sections // 2
    low = section < half
    inner = jnp.logical_and(section >= half // 4, section < half - half // 4)
    depth = lax.rem(me, 4)
    eighth = lax.rem(section // (sections // 8), 4)
    at_middle = jnp.logical_or(eighth == 0, eighth == 3)
    act_first = jnp.logical_and(low, jnp.logical_not(inner))
    act_mid = jnp.logical_and(inner, depth < 2)
    act_later = jnp.logical_and(inner, depth >= 2)

    def cols(h):
        return pl.ds(pl.multiple_of(h * HD, HD), HD)

    def each_head(f):
        def step(h, c):
            f(h)
            return c

        lax.fori_loop(0, heads, step, 0)

    def each_peer(start, f):
        def step(p, c):
            f(p)
            return c

        lax.fori_loop(start, width, step, 0)

    def remote(src, dst, send, recv, device):
        return pltpu.make_async_remote_copy(
            src_ref=src, dst_ref=dst, send_sem=send, recv_sem=recv,
            device_id=device, device_id_type=MESH,
        )

    def signal(sem, device):
        pl.semaphore_signal(sem, inc=1, device_id=device, device_id_type=MESH)

    def held_copy(h):
        return remote(held.at[0, :, cols(h)], ss.at[h], held_send.at[h], held_recv.at[h], (mirror, me))

    def act_copy(h):
        return remote(act.at[0, :, cols(h)], far.at[h], far_send.at[h], far_recv.at[h], (mirror, me))

    def y_copy(h):
        return remote(ys.at[h], act_out.at[0, :, cols(h)], y_send.at[h], y_recv.at[h], (nxt, me))

    def b_copy(h):
        return remote(bo.at[h], grad_out.at[0, :, cols(h)], b_send.at[h], b_recv.at[h], (prv, me))

    def sum_copy(msg, gat, send, recv, p):
        return remote(msg, gat.at[me], send.at[p], recv.at[p], (section, lax.rem(me + p, width)))

    row, spot = me // 4, lax.rem(me, 4)

    def along_x(p):
        return remote(msg3, gat3.at[row], s3.at[p], r3.at[p], (section, lax.rem(row + p, 4) * 4 + spot))

    def along_z(p):
        return remote(msg4, gat4.at[spot], s3.at[p + 4], r3.at[p + 4], (section, row * 4 + lax.rem(spot + p, 4)))

    hsum_copy = remote(hsum, hsum_got, hs_send, hs_recv, (mirror, me))
    esum_copy = remote(esum, esum_got, es, er, (nxt, me))
    rate_copy = remote(rate_e, rate_e_got, rs, rr, (prv, me))

    barrier = pltpu.get_barrier_semaphore()

    @pl.when(odd)
    def _():
        signal(barrier, (mirror, me))
        signal(barrier, (prv, me))

        @pl.when(jnp.logical_not(last))
        def _():
            signal(barrier, (nxt, me))

        each_peer(1, lambda p: signal(barrier, (section, lax.rem(me + p, width))))

    load_held = pltpu.make_async_copy(held.at[0], hs, load_h)
    load_act = pltpu.make_async_copy(act.at[0], xs, load_x)
    load_grad = pltpu.make_async_copy(grad.at[0], gs, load_g)
    load_park = pltpu.make_async_copy(park, flags, load_p)
    load_gains = [
        pltpu.make_async_copy(src, dst, load_w.at[i])
        for i, (src, dst) in enumerate(((gq_in, gq), (gk_in, gk), (gv_in, gv)))
    ]
    load_held.start()
    load_act.start()
    load_grad.start()
    for copy in load_gains:
        copy.start()
    load_park.start()

    def squares(ref):
        def step(h, acc):
            v = ref[:, cols(h)].astype(F32)
            return acc + v * v

        return row_sums(lax.fori_loop(0, heads, step, jnp.zeros((SEQ, HD), F32)))

    load_held.wait()
    b0, b1 = squares(hs)
    hsum[0:1] = b0
    hsum[1:2] = b1

    def start_acts():
        @pl.when(act_first)
        def _():
            each_head(lambda h: act_copy(h).start())

    def start_some(h, c):
        held_copy(h).start()
        return c

    @pl.when(even)
    def _():
        pl.semaphore_wait(barrier, jnp.where(first, 2, 3))
        signal(hello, (mirror, me))
        signal(hello, (nxt, me))

        @pl.when(jnp.logical_not(first))
        def _():
            signal(hello, (prv, me))

        hsum_copy.start()
        some = jnp.where(at_middle, FIRST_MIDDLE, FIRST_BEHIND)
        lax.fori_loop(0, some, start_some, 0)
        pl.semaphore_wait(near, 1)
        lax.fori_loop(some, heads, start_some, 0)
        start_acts()

    @pl.when(odd)
    def _():
        pl.semaphore_wait(hello, jnp.where(last, 2, 3))
        hsum_copy.start()
        signal(near, (prv, me))
        lax.fori_loop(0, heads, start_some, 0)
        start_acts()

    load_act.wait()
    a0, a1 = squares(xs)
    for copy in load_gains:
        copy.wait()
    load_park.wait()
    flag = flags[mirror]

    @pl.when(even)
    def _():
        esum[0:1] = a0
        esum[1:2] = a1
        hsum_copy.wait_recv()
        esum[2:4] = hsum_got[...]
        esum_copy.start()
        rate_copy.wait_recv()

    @pl.when(odd)
    def _():
        pl.semaphore_wait(barrier, width - 1)
        msg1[0:1] = a0
        msg1[1:2] = a1
        hsum_copy.wait_recv()
        msg1[2:4] = hsum_got[...]
        esum_copy.wait_recv()
        msg1[4:8] = esum_got[...]
        each_peer(1, lambda p: sum_copy(msg1, gat1, s1, r1, p).start())
        gat1[pl.ds(me, 1)] = msg1[...][None]
        each_peer(1, lambda p: sum_copy(msg1, gat1, s1, r1, p).wait_recv())
        rates = lax.rsqrt(jnp.sum(gat1[...], axis=0) / features + EPS)
        rate_e[...] = rates[4:8]
        rate_copy.start()
        rate_e_got[...] = rates[0:4]

    rates = rate_e_got[...]
    rate_f[pl.ds(0, 128)] = as_column(rates[0:1])
    rate_f[pl.ds(128, 128)] = as_column(rates[1:2])
    rate_s[pl.ds(0, 128)] = as_column(rates[2:3])
    rate_s[pl.ds(128, 128)] = as_column(rates[3:4])

    def project(xf, rate, h):
        normed = xf * rate
        return (
            (normed * gq[:, cols(h)]).astype(BF16),
            (normed * gk[:, cols(h)]).astype(BF16),
            (normed * gv[:, cols(h)]).astype(BF16),
        )

    tacc[...] = jnp.zeros((SEQ, HD), F32)

    def backward(h):
        held_copy(h).wait_recv()

        xf = ss[h].astype(F32)
        rate = rate_s[...]
        q, k, v = project(xf, rate, h)
        g = gs[:, cols(h)]
        p0 = softmax_rows(nt(q[0:128], k[0:128]), 0)
        p1 = softmax_rows(nt(q[128:256], k), 128)
        d0 = nt(g[0:128], v[0:128])
        d1 = nt(g[128:256], v)

        def dscore(probs, dprob):
            delta = jnp.sum(probs * dprob, axis=-1, keepdims=True)
            return (probs * (dprob - delta) * SCALE).astype(BF16)

        e0 = dscore(p0, d0)
        e1 = dscore(p1, d1)
        dval = tn(p1.astype(BF16), g[128:256])
        dkey = tn(e1, q[128:256])
        dval0 = dval[0:128] + tn(p0.astype(BF16), g[0:128])
        dkey0 = dkey[0:128] + tn(e0, q[0:128])
        g_q, g_k, g_v = gq[:, cols(h)], gk[:, cols(h)], gv[:, cols(h)]
        dn0 = nn(e0, k[0:128]) * g_q + dkey0 * g_k + dval0 * g_v
        dn1 = nn(e1, k) * g_q + dkey[128:256] * g_k + dval[128:256] * g_v
        zs[h, pl.ds(0, 128)] = g[0:128].astype(F32) + rate[0:128] * dn0
        zs[h, pl.ds(128, 128)] = g[128:256].astype(F32) + rate[128:256] * dn1
        tacc[pl.ds(0, 128)] += dn0 * xf[0:128]
        tacc[pl.ds(128, 128)] += dn1 * xf[128:256]

    @pl.when(act_mid)
    def _():
        each_head(lambda h: act_copy(h).start())

    load_grad.wait()
    each_head(backward)

    t0, t1 = row_sums(tacc[...])
    msg3[0:1] = t0
    msg3[1:2] = t1
    for p in range(1, 4):
        along_x(p).start()
    gat3[pl.ds(row, 1)] = msg3[...][None]
    def forward(h):
        xf = xs[:, cols(h)].astype(F32)
        q, k, v = project(xf, rate_f[...], h)
        p0 = softmax_rows(nt(q[0:128], k[0:128]), 0).astype(BF16)
        p1 = softmax_rows(nt(q[128:256], k), 128).astype(BF16)
        ys[h, pl.ds(0, 128)] = (xf[0:128] + nn(p0, v[0:128])).astype(BF16)
        ys[h, pl.ds(128, 128)] = (xf[128:256] + nn(p1, v)).astype(BF16)

        @pl.when(jnp.logical_and(jnp.logical_not(last), h >= 3))
        def _():
            y_copy(h).start()

    lax.fori_loop(0, 3, lambda h, c: (forward(h), c)[1], 0)

    for p in range(1, 4):
        along_x(p).wait_recv()
    mid = jnp.sum(gat3[...], axis=0)
    msg4[...] = mid
    for p in range(1, 4):
        along_z(p).start()
    gat4[pl.ds(spot, 1)] = mid[None]

    @pl.when(jnp.logical_not(last))
    def _():
        lax.fori_loop(0, min(3, heads), lambda h, c: (y_copy(h).start(), c)[1], 0)

    lax.fori_loop(3, heads, lambda h, c: (forward(h), c)[1], 0)

    @pl.when(act_later)
    def _():
        each_head(lambda h: act_copy(h).start())

    def zero_grad(h):
        return pltpu.make_async_copy(xn.at[h], grad_out.at[0, :, cols(h)], zero_sem.at[h])

    def held_place(h):
        return pltpu.make_async_copy(ho.at[h], held_out.at[0, :, cols(h)], ho_sem.at[h])

    for p in range(1, 4):
        along_z(p).wait_recv()
    totals = jnp.sum(gat4[...], axis=0) / features
    rate_f[pl.ds(0, 128)] = as_column(totals[0:1])
    rate_f[pl.ds(128, 128)] = as_column(totals[1:2])
    rate = rate_s[...]
    rate_f[...] = rate_f[...] * (rate * rate * rate)

    def finish(h):
        bo[h] = (zs[h] - ss[h].astype(F32) * rate_f[...]).astype(BF16)

        @pl.when(jnp.logical_not(first))
        def _():
            b_copy(h).start()

    each_head(finish)

    @pl.when(last)
    def _():
        def zero(h):
            xn[h] = jnp.zeros((SEQ, HD), BF16)
            zero_grad(h).start()

        each_head(zero)

    def zero_place(h):
        return pltpu.make_async_copy(xn.at[h], act_out.at[0, :, cols(h)], zero_sem.at[h])

    @pl.when(first)
    def _():
        def zero(h):
            xn[h] = jnp.zeros((SEQ, HD), BF16)
            zero_place(h).start()

        each_head(zero)

    def place(h):
        @pl.when(jnp.logical_not(low))
        def _():
            act_copy(h).wait_recv()

        mine = hs[:, cols(h)]

        @pl.when(low)
        def _():
            ho[h] = mine

        @pl.when(jnp.logical_not(low))
        def _():
            ho[h] = jnp.where(flag == 1, far[h], mine)

        held_place(h).start()

    each_head(place)

    def drain(h):
        held_place(h).wait()
        held_copy(h).wait_send()

        @pl.when(first)
        def _():
            zero_place(h).wait()

        @pl.when(last)
        def _():
            zero_grad(h).wait()

        @pl.when(low)
        def _():
            act_copy(h).wait_send()

        @pl.when(jnp.logical_not(last))
        def _():
            y_copy(h).wait_send()
            b_copy(h).wait_recv()

        @pl.when(jnp.logical_not(first))
        def _():
            y_copy(h).wait_recv()
            b_copy(h).wait_send()

    each_head(drain)

    for p in range(1, 4):
        along_x(p).wait_send()
        along_z(p).wait_send()

    hsum_copy.wait_send()

    @pl.when(even)
    def _():
        esum_copy.wait_send()

    @pl.when(odd)
    def _():
        each_peer(1, lambda p: sum_copy(msg1, gat1, s1, r1, p).wait_send())
        rate_copy.wait_send()


def place_kernel(a, b, c, a_out, b_out, c_out, a_mid, b_mid, c_mid, sems):
    stages = ((a, a_mid, a_out), (b, b_mid, b_out), (c, c_mid, c_out))
    into = [pltpu.make_async_copy(src, mid, sems.at[0, i]) for i, (src, mid, _) in enumerate(stages)]
    outof = [pltpu.make_async_copy(mid, dst, sems.at[1, i]) for i, (_, mid, dst) in enumerate(stages)]
    for copy in into:
        copy.start()
    for first, second in zip(into, outof):
        first.wait()
        second.start()
    for copy in outof:
        copy.wait()


def solution(mesh):
    sections, width = mesh.shape["pipe"], mesh.shape["tp"]

    def shards(act_in, grad_in, held, park, gain_q, gain_k, gain_v):
        heads = act_in.shape[2] // HD
        block = jax.ShapeDtypeStruct(act_in.shape, BF16)
        hbm = pl.BlockSpec(memory_space=pltpu.HBM)
        dma = pltpu.SemaphoreType.DMA

        def body(*refs):
            kernel(heads, sections, width, *refs)

        per_head = [dma((heads,)), dma((heads,))]
        per_peer = [dma((width,)), dma((width,))]
        field = pltpu.VMEM((SEQ, HD), F32)
        rows = pltpu.VMEM((4, 128), F32)
        pair = pltpu.VMEM((2, 128), F32)
        four = pltpu.VMEM((4, 2, 128), F32)
        flat = pltpu.VMEM((SEQ, heads * HD), BF16)
        stack = pltpu.VMEM((heads, SEQ, HD), BF16)
        wide_stack = pltpu.VMEM((heads, SEQ, HD), F32)
        gain_row = pltpu.VMEM((1, heads * HD), F32)
        outs = pl.pallas_call(
            body,
            out_shape=(block, block, block),
            in_specs=[hbm] * 7,
            out_specs=(hbm, hbm, hbm),
            scratch_shapes=[
                flat, flat, flat, stack, stack, stack,
                wide_stack, stack,
                gain_row, gain_row, gain_row, pltpu.SMEM((sections,), jnp.int32),
                field, field, field,
                pltpu.VMEM((8, 128), F32), pltpu.VMEM((width, 8, 128), F32), pair, four, pair, four,
                pair, pair, rows, rows, rows, rows,
                stack, stack,
                dma, dma, dma, dma, dma((3,)),
                *per_head, *per_head, *per_head, *per_head,
                *per_peer, *per_peer,
                dma, dma, dma, dma, dma, dma,
                dma((heads,)), dma((heads,)),
                pltpu.SemaphoreType.REGULAR, pltpu.SemaphoreType.REGULAR,
            ],
            compiler_params=pltpu.CompilerParams(
                collective_id=0, has_side_effects=True, vmem_limit_bytes=56 * 1024 * 1024
            ),
            name="relay_tick",
        )(act_in, grad_in, held, park, gain_q, gain_k, gain_v)
        return pl.pallas_call(
            place_kernel,
            out_shape=(block, block, block),
            in_specs=[hbm] * 3,
            out_specs=(hbm, hbm, hbm),
            scratch_shapes=[pltpu.VMEM(block.shape, BF16)] * 3 + [dma((2, 3))],
            compiler_params=pltpu.CompilerParams(vmem_limit_bytes=56 * 1024 * 1024),
            name="place",
        )(*outs)

    wide = P("pipe", None, "tp")
    gain = P("pipe", "tp")
    return jax.shard_map(
        shards,
        mesh=mesh,
        in_specs=(wide, wide, wide, P(), gain, gain, gain),
        out_specs=(wide, wide, wide),
        check_vma=False,
    )
```

```python
import jax
import jax.numpy as jnp
from jax import lax
from jax.experimental import pallas as pl
from jax.experimental.pallas import tpu as pltpu
from jax.sharding import PartitionSpec as P

HD = 128
SEQ = 256
EPS = 1e-05
MESH = pl.DeviceIdType.MESH
F32 = jnp.float32
BF16 = jnp.bfloat16
SCALE = HD ** (-0.5)
FIRST_MIDDLE = 1
FIRST_BEHIND = 3


def nt(a, b):
    return lax.dot_general(a, b, (((1,), (1,)), ((), ())), preferred_element_type=F32)


def tn(a, b):
    return lax.dot_general(a, b, (((0,), (0,)), ((), ())), preferred_element_type=F32)


def nn(a, b):
    return lax.dot_general(a, b, (((1,), (0,)), ((), ())), preferred_element_type=F32)


def row_sums(field):
    ones = jnp.ones((8, HD), F32)
    sums = lax.dot_general(
        ones, field, (((1,), (1,)), ((), ())),
        precision=lax.Precision.HIGHEST, preferred_element_type=F32,
    )
    return sums[0:1, 0:128], sums[0:1, 128:256]


def as_column(row):
    return jnp.transpose(jnp.broadcast_to(row, (128, 128)))


def softmax_rows(raw, first_row):
    rows = lax.broadcasted_iota(jnp.int32, raw.shape, 0) + first_row
    columns = lax.broadcasted_iota(jnp.int32, raw.shape, 1)
    raw = jnp.where(rows >= columns, raw * SCALE, -jnp.inf)
    top = jnp.max(raw, axis=-1, keepdims=True)
    powers = jnp.exp(raw - top)
    return powers * (1.0 / jnp.sum(powers, axis=-1, keepdims=True))


def kernel(
    heads, sections, width,
    act, grad, held, park, gq_in, gk_in, gv_in,
    act_out, grad_out, held_out,
    xs, gs, hs, ss, ys, xn, zs, far, gq, gk, gv, flags,
    rate_f, rate_s, tacc,
    msg1, gat1, msg3, gat3, msg4, gat4, hsum, hsum_got, esum, esum_got, rate_e, rate_e_got, bo, ho,
    load_x, load_g, load_h, load_p, load_w,
    held_send, held_recv, y_send, y_recv, b_send, b_recv, far_send, far_recv,
    s1, r1, s3, r3, hs_send, hs_recv, es, er, rs, rr, ho_sem, zero_sem,
    hello, near,
):
    section = lax.axis_index("pipe")
    me = lax.axis_index("tp")
    mirror = sections - 1 - section
    nxt = jnp.minimum(section + 1, sections - 1)
    prv = jnp.maximum(section - 1, 0)
    features = width * heads * HD
    odd = lax.rem(section, 2) == 1
    even = lax.rem(section, 2) == 0
    first = section == 0
    last = section == sections - 1
    half = sections // 2
    low = section < half
    inner = jnp.logical_and(section >= half // 4, section < half - half // 4)
    depth = lax.rem(me, 4)
    eighth = lax.rem(section // (sections // 8), 4)
    at_middle = jnp.logical_or(eighth == 0, eighth == 3)
    act_first = jnp.logical_and(low, jnp.logical_not(inner))
    act_mid = jnp.logical_and(inner, depth < 2)
    act_later = jnp.logical_and(inner, depth >= 2)

    def cols(h):
        return pl.ds(pl.multiple_of(h * HD, HD), HD)

    def each_head(f):
        def step(h, c):
            f(h)
            return c

        lax.fori_loop(0, heads, step, 0)

    def each_peer(start, f):
        def step(p, c):
            f(p)
            return c

        lax.fori_loop(start, width, step, 0)

    def remote(src, dst, send, recv, device):
        return pltpu.make_async_remote_copy(
            src_ref=src, dst_ref=dst, send_sem=send, recv_sem=recv,
            device_id=device, device_id_type=MESH,
        )

    def signal(sem, device):
        pl.semaphore_signal(sem, inc=1, device_id=device, device_id_type=MESH)

    def held_copy(h):
        return remote(held.at[0, :, cols(h)], ss.at[h], held_send.at[h], held_recv.at[h], (mirror, me))

    def act_copy(h):
        return remote(act.at[0, :, cols(h)], far.at[h], far_send.at[h], far_recv.at[h], (mirror, me))

    def y_copy(h):
        return remote(ys.at[h], act_out.at[0, :, cols(h)], y_send.at[h], y_recv.at[h], (nxt, me))

    def b_copy(h):
        return remote(bo.at[h], grad_out.at[0, :, cols(h)], b_send.at[h], b_recv.at[h], (prv, me))

    def sum_copy(msg, gat, send, recv, p):
        return remote(msg, gat.at[me], send.at[p], recv.at[p], (section, lax.rem(me + p, width)))

    row, spot = me // 4, lax.rem(me, 4)

    def along_x(p):
        return remote(msg3, gat3.at[row], s3.at[p], r3.at[p], (section, lax.rem(row + p, 4) * 4 + spot))

    def along_z(p):
        return remote(msg4, gat4.at[spot], s3.at[p + 4], r3.at[p + 4], (section, row * 4 + lax.rem(spot + p, 4)))

    hsum_copy = remote(hsum, hsum_got, hs_send, hs_recv, (mirror, me))
    esum_copy = remote(esum, esum_got, es, er, (nxt, me))
    rate_copy = remote(rate_e, rate_e_got, rs, rr, (prv, me))

    barrier = pltpu.get_barrier_semaphore()

    @pl.when(odd)
    def _():
        signal(barrier, (mirror, me))
        signal(barrier, (prv, me))

        @pl.when(jnp.logical_not(last))
        def _():
            signal(barrier, (nxt, me))

        each_peer(1, lambda p: signal(barrier, (section, lax.rem(me + p, width))))

    load_held = pltpu.make_async_copy(held.at[0], hs, load_h)
    load_act = pltpu.make_async_copy(act.at[0], xs, load_x)
    load_grad = pltpu.make_async_copy(grad.at[0], gs, load_g)
    load_park = pltpu.make_async_copy(park, flags, load_p)
    load_gains = [
        pltpu.make_async_copy(src, dst, load_w.at[i])
        for i, (src, dst) in enumerate(((gq_in, gq), (gk_in, gk), (gv_in, gv)))
    ]
    load_held.start()
    load_act.start()
    load_grad.start()
    for copy in load_gains:
        copy.start()
    load_park.start()

    def squares(ref):
        def step(h, acc):
            v = ref[:, cols(h)].astype(F32)
            return acc + v * v

        return row_sums(lax.fori_loop(0, heads, step, jnp.zeros((SEQ, HD), F32)))

    load_held.wait()
    b0, b1 = squares(hs)
    hsum[0:1] = b0
    hsum[1:2] = b1

    def start_acts():
        @pl.when(act_first)
        def _():
            each_head(lambda h: act_copy(h).start())

    def start_some(h, c):
        held_copy(h).start()
        return c

    @pl.when(even)
    def _():
        pl.semaphore_wait(barrier, jnp.where(first, 2, 3))
        signal(hello, (mirror, me))
        signal(hello, (nxt, me))

        @pl.when(jnp.logical_not(first))
        def _():
            signal(hello, (prv, me))

        hsum_copy.start()
        some = jnp.where(at_middle, FIRST_MIDDLE, FIRST_BEHIND)
        lax.fori_loop(0, some, start_some, 0)
        pl.semaphore_wait(near, 1)
        lax.fori_loop(some, heads, start_some, 0)
        start_acts()

    @pl.when(odd)
    def _():
        pl.semaphore_wait(hello, jnp.where(last, 2, 3))
        hsum_copy.start()
        signal(near, (prv, me))
        lax.fori_loop(0, heads, start_some, 0)
        start_acts()

    load_act.wait()
    a0, a1 = squares(xs)
    for copy in load_gains:
        copy.wait()
    load_park.wait()
    flag = flags[mirror]

    @pl.when(even)
    def _():
        esum[0:1] = a0
        esum[1:2] = a1
        hsum_copy.wait_recv()
        esum[2:4] = hsum_got[...]
        esum_copy.start()
        rate_copy.wait_recv()

    @pl.when(odd)
    def _():
        pl.semaphore_wait(barrier, width - 1)
        msg1[0:1] = a0
        msg1[1:2] = a1
        hsum_copy.wait_recv()
        msg1[2:4] = hsum_got[...]
        esum_copy.wait_recv()
        msg1[4:8] = esum_got[...]
        each_peer(1, lambda p: sum_copy(msg1, gat1, s1, r1, p).start())
        gat1[pl.ds(me, 1)] = msg1[...][None]
        each_peer(1, lambda p: sum_copy(msg1, gat1, s1, r1, p).wait_recv())
        rates = lax.rsqrt(jnp.sum(gat1[...], axis=0) / features + EPS)
        rate_e[...] = rates[4:8]
        rate_copy.start()
        rate_e_got[...] = rates[0:4]

    rates = rate_e_got[...]
    rate_f[pl.ds(0, 128)] = as_column(rates[0:1])
    rate_f[pl.ds(128, 128)] = as_column(rates[1:2])
    rate_s[pl.ds(0, 128)] = as_column(rates[2:3])
    rate_s[pl.ds(128, 128)] = as_column(rates[3:4])

    def project(xf, rate, h):
        normed = xf * rate
        return (
            (normed * gq[:, cols(h)]).astype(BF16),
            (normed * gk[:, cols(h)]).astype(BF16),
            (normed * gv[:, cols(h)]).astype(BF16),
        )

    tacc[...] = jnp.zeros((SEQ, HD), F32)

    def backward(h):
        held_copy(h).wait_recv()

        xf = ss[h].astype(F32)
        rate = rate_s[...]
        q, k, v = project(xf, rate, h)
        g = gs[:, cols(h)]
        p0 = softmax_rows(nt(q[0:128], k[0:128]), 0)
        p1 = softmax_rows(nt(q[128:256], k), 128)
        d0 = nt(g[0:128], v[0:128])
        d1 = nt(g[128:256], v)

        def dscore(probs, dprob):
            delta = jnp.sum(probs * dprob, axis=-1, keepdims=True)
            return (probs * (dprob - delta) * SCALE).astype(BF16)

        e0 = dscore(p0, d0)
        e1 = dscore(p1, d1)
        dval = tn(p1.astype(BF16), g[128:256])
        dkey = tn(e1, q[128:256])
        dval0 = dval[0:128] + tn(p0.astype(BF16), g[0:128])
        dkey0 = dkey[0:128] + tn(e0, q[0:128])
        g_q, g_k, g_v = gq[:, cols(h)], gk[:, cols(h)], gv[:, cols(h)]
        dn0 = nn(e0, k[0:128]) * g_q + dkey0 * g_k + dval0 * g_v
        dn1 = nn(e1, k) * g_q + dkey[128:256] * g_k + dval[128:256] * g_v
        zs[h, pl.ds(0, 128)] = g[0:128].astype(F32) + rate[0:128] * dn0
        zs[h, pl.ds(128, 128)] = g[128:256].astype(F32) + rate[128:256] * dn1
        tacc[pl.ds(0, 128)] += dn0 * xf[0:128]
        tacc[pl.ds(128, 128)] += dn1 * xf[128:256]

    @pl.when(act_mid)
    def _():
        each_head(lambda h: act_copy(h).start())

    load_grad.wait()
    each_head(backward)

    t0, t1 = row_sums(tacc[...])
    msg3[0:1] = t0
    msg3[1:2] = t1
    for p in range(1, 4):
        along_x(p).start()
    gat3[pl.ds(row, 1)] = msg3[...][None]
    def forward(h):
        xf = xs[:, cols(h)].astype(F32)
        q, k, v = project(xf, rate_f[...], h)
        p0 = softmax_rows(nt(q[0:128], k[0:128]), 0).astype(BF16)
        p1 = softmax_rows(nt(q[128:256], k), 128).astype(BF16)
        ys[h, pl.ds(0, 128)] = (xf[0:128] + nn(p0, v[0:128])).astype(BF16)
        ys[h, pl.ds(128, 128)] = (xf[128:256] + nn(p1, v)).astype(BF16)

        @pl.when(jnp.logical_and(jnp.logical_not(last), h >= 3))
        def _():
            y_copy(h).start()

    lax.fori_loop(0, 3, lambda h, c: (forward(h), c)[1], 0)

    for p in range(1, 4):
        along_x(p).wait_recv()
    mid = jnp.sum(gat3[...], axis=0)
    msg4[...] = mid
    for p in range(1, 4):
        along_z(p).start()
    gat4[pl.ds(spot, 1)] = mid[None]

    @pl.when(jnp.logical_not(last))
    def _():
        lax.fori_loop(0, min(3, heads), lambda h, c: (y_copy(h).start(), c)[1], 0)

    lax.fori_loop(3, heads, lambda h, c: (forward(h), c)[1], 0)

    @pl.when(act_later)
    def _():
        each_head(lambda h: act_copy(h).start())

    def zero_grad(h):
        return pltpu.make_async_copy(xn.at[h], grad_out.at[0, :, cols(h)], zero_sem.at[h])

    def held_place(h):
        return pltpu.make_async_copy(ho.at[h], held_out.at[0, :, cols(h)], ho_sem.at[h])

    for p in range(1, 4):
        along_z(p).wait_recv()
    totals = jnp.sum(gat4[...], axis=0) / features
    rate_f[pl.ds(0, 128)] = as_column(totals[0:1])
    rate_f[pl.ds(128, 128)] = as_column(totals[1:2])
    rate = rate_s[...]
    rate_f[...] = rate_f[...] * (rate * rate * rate)

    def finish(h):
        bo[h] = (zs[h] - ss[h].astype(F32) * rate_f[...]).astype(BF16)

        @pl.when(jnp.logical_not(first))
        def _():
            b_copy(h).start()

    each_head(finish)

    @pl.when(last)
    def _():
        def zero(h):
            xn[h] = jnp.zeros((SEQ, HD), BF16)
            zero_grad(h).start()

        each_head(zero)

    def zero_place(h):
        return pltpu.make_async_copy(xn.at[h], act_out.at[0, :, cols(h)], zero_sem.at[h])

    @pl.when(first)
    def _():
        def zero(h):
            xn[h] = jnp.zeros((SEQ, HD), BF16)
            zero_place(h).start()

        each_head(zero)

    def place(h):
        @pl.when(jnp.logical_not(low))
        def _():
            act_copy(h).wait_recv()

        mine = hs[:, cols(h)]

        @pl.when(low)
        def _():
            ho[h] = mine

        @pl.when(jnp.logical_not(low))
        def _():
            ho[h] = jnp.where(flag == 1, far[h], mine)

        held_place(h).start()

    each_head(place)

    def drain(h):
        held_place(h).wait()
        held_copy(h).wait_send()

        @pl.when(first)
        def _():
            zero_place(h).wait()

        @pl.when(last)
        def _():
            zero_grad(h).wait()

        @pl.when(low)
        def _():
            act_copy(h).wait_send()

        @pl.when(jnp.logical_not(last))
        def _():
            y_copy(h).wait_send()
            b_copy(h).wait_recv()

        @pl.when(jnp.logical_not(first))
        def _():
            y_copy(h).wait_recv()
            b_copy(h).wait_send()

    each_head(drain)

    for p in range(1, 4):
        along_x(p).wait_send()
        along_z(p).wait_send()

    hsum_copy.wait_send()

    @pl.when(even)
    def _():
        esum_copy.wait_send()

    @pl.when(odd)
    def _():
        each_peer(1, lambda p: sum_copy(msg1, gat1, s1, r1, p).wait_send())
        rate_copy.wait_send()


def place_kernel(a, b, c, a_out, b_out, c_out, a_mid, b_mid, c_mid, sems):
    stages = ((a, a_mid, a_out), (b, b_mid, b_out), (c, c_mid, c_out))
    into = [pltpu.make_async_copy(src, mid, sems.at[0, i]) for i, (src, mid, _) in enumerate(stages)]
    outof = [pltpu.make_async_copy(mid, dst, sems.at[1, i]) for i, (_, mid, dst) in enumerate(stages)]
    for copy in into:
        copy.start()
    for first, second in zip(into, outof):
        first.wait()
        second.start()
    for copy in outof:
        copy.wait()


def solution(mesh):
    sections, width = mesh.shape["pipe"], mesh.shape["tp"]

    def shards(act_in, grad_in, held, park, gain_q, gain_k, gain_v):
        heads = act_in.shape[2] // HD
        block = jax.ShapeDtypeStruct(act_in.shape, BF16)
        hbm = pl.BlockSpec(memory_space=pltpu.HBM)
        dma = pltpu.SemaphoreType.DMA

        def body(*refs):
            kernel(heads, sections, width, *refs)

        per_head = [dma((heads,)), dma((heads,))]
        per_peer = [dma((width,)), dma((width,))]
        field = pltpu.VMEM((SEQ, HD), F32)
        rows = pltpu.VMEM((4, 128), F32)
        pair = pltpu.VMEM((2, 128), F32)
        four = pltpu.VMEM((4, 2, 128), F32)
        flat = pltpu.VMEM((SEQ, heads * HD), BF16)
        stack = pltpu.VMEM((heads, SEQ, HD), BF16)
        wide_stack = pltpu.VMEM((heads, SEQ, HD), F32)
        gain_row = pltpu.VMEM((1, heads * HD), F32)
        outs = pl.pallas_call(
            body,
            out_shape=(block, block, block),
            in_specs=[hbm] * 7,
            out_specs=(hbm, hbm, hbm),
            scratch_shapes=[
                flat, flat, flat, stack, stack, stack,
                wide_stack, stack,
                gain_row, gain_row, gain_row, pltpu.SMEM((sections,), jnp.int32),
                field, field, field,
                pltpu.VMEM((8, 128), F32), pltpu.VMEM((width, 8, 128), F32), pair, four, pair, four,
                pair, pair, rows, rows, rows, rows,
                stack, stack,
                dma, dma, dma, dma, dma((3,)),
                *per_head, *per_head, *per_head, *per_head,
                *per_peer, *per_peer,
                dma, dma, dma, dma, dma, dma,
                dma((heads,)), dma((heads,)),
                pltpu.SemaphoreType.REGULAR, pltpu.SemaphoreType.REGULAR,
            ],
            compiler_params=pltpu.CompilerParams(
                collective_id=0, has_side_effects=True, vmem_limit_bytes=56 * 1024 * 1024
            ),
            name="relay_tick",
        )(act_in, grad_in, held, park, gain_q, gain_k, gain_v)
        return pl.pallas_call(
            place_kernel,
            out_shape=(block, block, block),
            in_specs=[hbm] * 3,
            out_specs=(hbm, hbm, hbm),
            scratch_shapes=[pltpu.VMEM(block.shape, BF16)] * 3 + [dma((2, 3))],
            compiler_params=pltpu.CompilerParams(vmem_limit_bytes=56 * 1024 * 1024),
            name="place",
        )(*outs)

    wide = P("pipe", None, "tp")
    gain = P("pipe", "tp")
    return jax.shard_map(
        shards,
        mesh=mesh,
        in_specs=(wide, wide, wide, P(), gain, gain, gain),
        out_specs=(wide, wide, wide),
        check_vma=False,
    )
```

```python
import jax
import jax.numpy as jnp
from jax import lax
from jax.experimental import pallas as pl
from jax.experimental.pallas import tpu as pltpu
from jax.sharding import PartitionSpec as P

HD = 128
SEQ = 256
EPS = 1e-05
MESH = pl.DeviceIdType.MESH
F32 = jnp.float32
BF16 = jnp.bfloat16
SCALE = HD ** (-0.5)
FIRST_MIDDLE = 1
FIRST_BEHIND = 4


def nt(a, b):
    return lax.dot_general(a, b, (((1,), (1,)), ((), ())), preferred_element_type=F32)


def tn(a, b):
    return lax.dot_general(a, b, (((0,), (0,)), ((), ())), preferred_element_type=F32)


def nn(a, b):
    return lax.dot_general(a, b, (((1,), (0,)), ((), ())), preferred_element_type=F32)


def row_sums(field):
    ones = jnp.ones((8, HD), F32)
    sums = lax.dot_general(
        ones, field, (((1,), (1,)), ((), ())),
        precision=lax.Precision.HIGHEST, preferred_element_type=F32,
    )
    return sums[0:1, 0:128], sums[0:1, 128:256]


def as_column(row):
    return jnp.transpose(jnp.broadcast_to(row, (128, 128)))


def softmax_rows(raw, first_row):
    rows = lax.broadcasted_iota(jnp.int32, raw.shape, 0) + first_row
    columns = lax.broadcasted_iota(jnp.int32, raw.shape, 1)
    raw = jnp.where(rows >= columns, raw * SCALE, -jnp.inf)
    top = jnp.max(raw, axis=-1, keepdims=True)
    powers = jnp.exp(raw - top)
    return powers * (1.0 / jnp.sum(powers, axis=-1, keepdims=True))


def kernel(
    heads, sections, width,
    act, grad, held, park, gq_in, gk_in, gv_in,
    act_out, grad_out, held_out,
    xs, gs, hs, ss, ys, xn, zs, far, gq, gk, gv, flags,
    rate_f, rate_s, tacc,
    msg1, gat1, msg3, gat3, msg4, gat4, hsum, hsum_got, esum, esum_got, rate_e, rate_e_got, bo, ho,
    load_x, load_g, load_h, load_p, load_w,
    held_send, held_recv, y_send, y_recv, b_send, b_recv, far_send, far_recv,
    s1, r1, s3, r3, hs_send, hs_recv, es, er, rs, rr, ho_sem, zero_sem,
    hello, near,
):
    section = lax.axis_index("pipe")
    me = lax.axis_index("tp")
    mirror = sections - 1 - section
    nxt = jnp.minimum(section + 1, sections - 1)
    prv = jnp.maximum(section - 1, 0)
    features = width * heads * HD
    odd = lax.rem(section, 2) == 1
    even = lax.rem(section, 2) == 0
    first = section == 0
    last = section == sections - 1
    half = sections // 2
    low = section < half
    inner = jnp.logical_and(section >= half // 4, section < half - half // 4)
    depth = lax.rem(me, 4)
    eighth = lax.rem(section // (sections // 8), 4)
    at_middle = jnp.logical_or(eighth == 0, eighth == 3)
    act_first = jnp.logical_and(low, jnp.logical_not(inner))
    act_mid = jnp.logical_and(inner, depth < 2)
    act_later = jnp.logical_and(inner, depth >= 2)

    def cols(h):
        return pl.ds(pl.multiple_of(h * HD, HD), HD)

    def each_head(f):
        def step(h, c):
            f(h)
            return c

        lax.fori_loop(0, heads, step, 0)

    def each_peer(start, f):
        def step(p, c):
            f(p)
            return c

        lax.fori_loop(start, width, step, 0)

    def remote(src, dst, send, recv, device):
        return pltpu.make_async_remote_copy(
            src_ref=src, dst_ref=dst, send_sem=send, recv_sem=recv,
            device_id=device, device_id_type=MESH,
        )

    def signal(sem, device):
        pl.semaphore_signal(sem, inc=1, device_id=device, device_id_type=MESH)

    def held_copy(h):
        return remote(held.at[0, :, cols(h)], ss.at[h], held_send.at[h], held_recv.at[h], (mirror, me))

    def act_copy(h):
        return remote(act.at[0, :, cols(h)], far.at[h], far_send.at[h], far_recv.at[h], (mirror, me))

    def y_copy(h):
        return remote(ys.at[h], act_out.at[0, :, cols(h)], y_send.at[h], y_recv.at[h], (nxt, me))

    def b_copy(h):
        return remote(bo.at[h], grad_out.at[0, :, cols(h)], b_send.at[h], b_recv.at[h], (prv, me))

    def sum_copy(msg, gat, send, recv, p):
        return remote(msg, gat.at[me], send.at[p], recv.at[p], (section, lax.rem(me + p, width)))

    row, spot = me // 4, lax.rem(me, 4)

    def along_x(p):
        return remote(msg3, gat3.at[row], s3.at[p], r3.at[p], (section, lax.rem(row + p, 4) * 4 + spot))

    def along_z(p):
        return remote(msg4, gat4.at[spot], s3.at[p + 4], r3.at[p + 4], (section, row * 4 + lax.rem(spot + p, 4)))

    hsum_copy = remote(hsum, hsum_got, hs_send, hs_recv, (mirror, me))
    esum_copy = remote(esum, esum_got, es, er, (nxt, me))
    rate_copy = remote(rate_e, rate_e_got, rs, rr, (prv, me))

    barrier = pltpu.get_barrier_semaphore()

    @pl.when(odd)
    def _():
        signal(barrier, (mirror, me))
        signal(barrier, (prv, me))

        @pl.when(jnp.logical_not(last))
        def _():
            signal(barrier, (nxt, me))

        each_peer(1, lambda p: signal(barrier, (section, lax.rem(me + p, width))))

    load_held = pltpu.make_async_copy(held.at[0], hs, load_h)
    load_act = pltpu.make_async_copy(act.at[0], xs, load_x)
    load_grad = pltpu.make_async_copy(grad.at[0], gs, load_g)
    load_park = pltpu.make_async_copy(park, flags, load_p)
    load_gains = [
        pltpu.make_async_copy(src, dst, load_w.at[i])
        for i, (src, dst) in enumerate(((gq_in, gq), (gk_in, gk), (gv_in, gv)))
    ]
    load_held.start()
    load_act.start()
    load_grad.start()
    for copy in load_gains:
        copy.start()
    load_park.start()

    def squares(ref):
        def step(h, acc):
            v = ref[:, cols(h)].astype(F32)
            return acc + v * v

        return row_sums(lax.fori_loop(0, heads, step, jnp.zeros((SEQ, HD), F32)))

    load_held.wait()
    b0, b1 = squares(hs)
    hsum[0:1] = b0
    hsum[1:2] = b1

    def start_acts():
        @pl.when(act_first)
        def _():
            each_head(lambda h: act_copy(h).start())

    def start_some(h, c):
        held_copy(h).start()
        return c

    @pl.when(even)
    def _():
        pl.semaphore_wait(barrier, jnp.where(first, 2, 3))
        signal(hello, (mirror, me))
        signal(hello, (nxt, me))

        @pl.when(jnp.logical_not(first))
        def _():
            signal(hello, (prv, me))

        hsum_copy.start()
        some = jnp.where(at_middle, FIRST_MIDDLE, FIRST_BEHIND)
        lax.fori_loop(0, some, start_some, 0)
        pl.semaphore_wait(near, 1)
        lax.fori_loop(some, heads, start_some, 0)
        start_acts()

    @pl.when(odd)
    def _():
        pl.semaphore_wait(hello, jnp.where(last, 2, 3))
        hsum_copy.start()
        signal(near, (prv, me))
        lax.fori_loop(0, heads, start_some, 0)
        start_acts()

    load_act.wait()
    a0, a1 = squares(xs)
    for copy in load_gains:
        copy.wait()
    load_park.wait()
    flag = flags[mirror]

    @pl.when(even)
    def _():
        esum[0:1] = a0
        esum[1:2] = a1
        hsum_copy.wait_recv()
        esum[2:4] = hsum_got[...]
        esum_copy.start()
        rate_copy.wait_recv()

    @pl.when(odd)
    def _():
        pl.semaphore_wait(barrier, width - 1)
        msg1[0:1] = a0
        msg1[1:2] = a1
        hsum_copy.wait_recv()
        msg1[2:4] = hsum_got[...]
        esum_copy.wait_recv()
        msg1[4:8] = esum_got[...]
        each_peer(1, lambda p: sum_copy(msg1, gat1, s1, r1, p).start())
        gat1[pl.ds(me, 1)] = msg1[...][None]
        each_peer(1, lambda p: sum_copy(msg1, gat1, s1, r1, p).wait_recv())
        rates = lax.rsqrt(jnp.sum(gat1[...], axis=0) / features + EPS)
        rate_e[...] = rates[4:8]
        rate_copy.start()
        rate_e_got[...] = rates[0:4]

    rates = rate_e_got[...]
    rate_f[pl.ds(0, 128)] = as_column(rates[0:1])
    rate_f[pl.ds(128, 128)] = as_column(rates[1:2])
    rate_s[pl.ds(0, 128)] = as_column(rates[2:3])
    rate_s[pl.ds(128, 128)] = as_column(rates[3:4])

    def project(xf, rate, h):
        normed = xf * rate
        return (
            (normed * gq[:, cols(h)]).astype(BF16),
            (normed * gk[:, cols(h)]).astype(BF16),
            (normed * gv[:, cols(h)]).astype(BF16),
        )

    tacc[...] = jnp.zeros((SEQ, HD), F32)

    def backward(h):
        held_copy(h).wait_recv()

        xf = ss[h].astype(F32)
        rate = rate_s[...]
        q, k, v = project(xf, rate, h)
        g = gs[:, cols(h)]
        p0 = softmax_rows(nt(q[0:128], k[0:128]), 0)
        p1 = softmax_rows(nt(q[128:256], k), 128)
        d0 = nt(g[0:128], v[0:128])
        d1 = nt(g[128:256], v)

        def dscore(probs, dprob):
            delta = jnp.sum(probs * dprob, axis=-1, keepdims=True)
            return (probs * (dprob - delta) * SCALE).astype(BF16)

        e0 = dscore(p0, d0)
        e1 = dscore(p1, d1)
        dval = tn(p1.astype(BF16), g[128:256])
        dkey = tn(e1, q[128:256])
        dval0 = dval[0:128] + tn(p0.astype(BF16), g[0:128])
        dkey0 = dkey[0:128] + tn(e0, q[0:128])
        g_q, g_k, g_v = gq[:, cols(h)], gk[:, cols(h)], gv[:, cols(h)]
        dn0 = nn(e0, k[0:128]) * g_q + dkey0 * g_k + dval0 * g_v
        dn1 = nn(e1, k) * g_q + dkey[128:256] * g_k + dval[128:256] * g_v
        zs[h, pl.ds(0, 128)] = g[0:128].astype(F32) + rate[0:128] * dn0
        zs[h, pl.ds(128, 128)] = g[128:256].astype(F32) + rate[128:256] * dn1
        tacc[pl.ds(0, 128)] += dn0 * xf[0:128]
        tacc[pl.ds(128, 128)] += dn1 * xf[128:256]

    @pl.when(act_mid)
    def _():
        each_head(lambda h: act_copy(h).start())

    load_grad.wait()
    each_head(backward)

    t0, t1 = row_sums(tacc[...])
    msg3[0:1] = t0
    msg3[1:2] = t1
    for p in range(1, 4):
        along_x(p).start()
    gat3[pl.ds(row, 1)] = msg3[...][None]
    def forward(h):
        xf = xs[:, cols(h)].astype(F32)
        q, k, v = project(xf, rate_f[...], h)
        p0 = softmax_rows(nt(q[0:128], k[0:128]), 0).astype(BF16)
        p1 = softmax_rows(nt(q[128:256], k), 128).astype(BF16)
        ys[h, pl.ds(0, 128)] = (xf[0:128] + nn(p0, v[0:128])).astype(BF16)
        ys[h, pl.ds(128, 128)] = (xf[128:256] + nn(p1, v)).astype(BF16)

        @pl.when(jnp.logical_and(jnp.logical_not(last), h >= 4))
        def _():
            y_copy(h).start()

    lax.fori_loop(0, 4, lambda h, c: (forward(h), c)[1], 0)

    for p in range(1, 4):
        along_x(p).wait_recv()
    mid = jnp.sum(gat3[...], axis=0)
    msg4[...] = mid
    for p in range(1, 4):
        along_z(p).start()
    gat4[pl.ds(spot, 1)] = mid[None]

    @pl.when(jnp.logical_not(last))
    def _():
        lax.fori_loop(0, 4, lambda h, c: (y_copy(h).start(), c)[1], 0)

    lax.fori_loop(4, heads, lambda h, c: (forward(h), c)[1], 0)

    @pl.when(act_later)
    def _():
        each_head(lambda h: act_copy(h).start())

    def zero_grad(h):
        return pltpu.make_async_copy(xn.at[h], grad_out.at[0, :, cols(h)], zero_sem.at[h])

    def held_place(h):
        return pltpu.make_async_copy(ho.at[h], held_out.at[0, :, cols(h)], ho_sem.at[h])

    for p in range(1, 4):
        along_z(p).wait_recv()
    totals = jnp.sum(gat4[...], axis=0) / features
    rate_f[pl.ds(0, 128)] = as_column(totals[0:1])
    rate_f[pl.ds(128, 128)] = as_column(totals[1:2])
    rate = rate_s[...]
    rate_f[...] = rate_f[...] * (rate * rate * rate)

    def finish(h):
        bo[h] = (zs[h] - ss[h].astype(F32) * rate_f[...]).astype(BF16)

        @pl.when(jnp.logical_not(first))
        def _():
            b_copy(h).start()

    each_head(finish)

    @pl.when(last)
    def _():
        def zero(h):
            xn[h] = jnp.zeros((SEQ, HD), BF16)
            zero_grad(h).start()

        each_head(zero)

    def zero_place(h):
        return pltpu.make_async_copy(xn.at[h], act_out.at[0, :, cols(h)], zero_sem.at[h])

    @pl.when(first)
    def _():
        def zero(h):
            xn[h] = jnp.zeros((SEQ, HD), BF16)
            zero_place(h).start()

        each_head(zero)

    def place(h):
        @pl.when(jnp.logical_not(low))
        def _():
            act_copy(h).wait_recv()

        mine = hs[:, cols(h)]

        @pl.when(low)
        def _():
            ho[h] = mine

        @pl.when(jnp.logical_not(low))
        def _():
            ho[h] = jnp.where(flag == 1, far[h], mine)

        held_place(h).start()

    each_head(place)

    def drain(h):
        held_place(h).wait()
        held_copy(h).wait_send()

        @pl.when(first)
        def _():
            zero_place(h).wait()

        @pl.when(last)
        def _():
            zero_grad(h).wait()

        @pl.when(low)
        def _():
            act_copy(h).wait_send()

        @pl.when(jnp.logical_not(last))
        def _():
            y_copy(h).wait_send()
            b_copy(h).wait_recv()

        @pl.when(jnp.logical_not(first))
        def _():
            y_copy(h).wait_recv()
            b_copy(h).wait_send()

    each_head(drain)

    for p in range(1, 4):
        along_x(p).wait_send()
        along_z(p).wait_send()

    hsum_copy.wait_send()

    @pl.when(even)
    def _():
        esum_copy.wait_send()

    @pl.when(odd)
    def _():
        each_peer(1, lambda p: sum_copy(msg1, gat1, s1, r1, p).wait_send())
        rate_copy.wait_send()


def place_kernel(a, b, c, a_out, b_out, c_out, a_mid, b_mid, c_mid, sems):
    stages = ((a, a_mid, a_out), (b, b_mid, b_out), (c, c_mid, c_out))
    into = [pltpu.make_async_copy(src, mid, sems.at[0, i]) for i, (src, mid, _) in enumerate(stages)]
    outof = [pltpu.make_async_copy(mid, dst, sems.at[1, i]) for i, (_, mid, dst) in enumerate(stages)]
    for copy in into:
        copy.start()
    for first, second in zip(into, outof):
        first.wait()
        second.start()
    for copy in outof:
        copy.wait()


def solution(mesh):
    sections, width = mesh.shape["pipe"], mesh.shape["tp"]

    def shards(act_in, grad_in, held, park, gain_q, gain_k, gain_v):
        heads = act_in.shape[2] // HD
        block = jax.ShapeDtypeStruct(act_in.shape, BF16)
        hbm = pl.BlockSpec(memory_space=pltpu.HBM)
        dma = pltpu.SemaphoreType.DMA

        def body(*refs):
            kernel(heads, sections, width, *refs)

        per_head = [dma((heads,)), dma((heads,))]
        per_peer = [dma((width,)), dma((width,))]
        field = pltpu.VMEM((SEQ, HD), F32)
        rows = pltpu.VMEM((4, 128), F32)
        pair = pltpu.VMEM((2, 128), F32)
        four = pltpu.VMEM((4, 2, 128), F32)
        flat = pltpu.VMEM((SEQ, heads * HD), BF16)
        stack = pltpu.VMEM((heads, SEQ, HD), BF16)
        wide_stack = pltpu.VMEM((heads, SEQ, HD), F32)
        gain_row = pltpu.VMEM((1, heads * HD), F32)
        outs = pl.pallas_call(
            body,
            out_shape=(block, block, block),
            in_specs=[hbm] * 7,
            out_specs=(hbm, hbm, hbm),
            scratch_shapes=[
                flat, flat, flat, stack, stack, stack,
                wide_stack, stack,
                gain_row, gain_row, gain_row, pltpu.SMEM((sections,), jnp.int32),
                field, field, field,
                pltpu.VMEM((8, 128), F32), pltpu.VMEM((width, 8, 128), F32), pair, four, pair, four,
                pair, pair, rows, rows, rows, rows,
                stack, stack,
                dma, dma, dma, dma, dma((3,)),
                *per_head, *per_head, *per_head, *per_head,
                *per_peer, *per_peer,
                dma, dma, dma, dma, dma, dma,
                dma((heads,)), dma((heads,)),
                pltpu.SemaphoreType.REGULAR, pltpu.SemaphoreType.REGULAR,
            ],
            compiler_params=pltpu.CompilerParams(
                collective_id=0, has_side_effects=True, vmem_limit_bytes=56 * 1024 * 1024
            ),
            name="relay_tick",
        )(act_in, grad_in, held, park, gain_q, gain_k, gain_v)
        return pl.pallas_call(
            place_kernel,
            out_shape=(block, block, block),
            in_specs=[hbm] * 3,
            out_specs=(hbm, hbm, hbm),
            scratch_shapes=[pltpu.VMEM(block.shape, BF16)] * 3 + [dma((2, 3))],
            compiler_params=pltpu.CompilerParams(vmem_limit_bytes=56 * 1024 * 1024),
            name="place",
        )(*outs)

    wide = P("pipe", None, "tp")
    gain = P("pipe", "tp")
    return jax.shard_map(
        shards,
        mesh=mesh,
        in_specs=(wide, wide, wide, P(), gain, gain, gain),
        out_specs=(wide, wide, wide),
        check_vma=False,
    )
```
